512 devices in a mesh: pop: 64 (over z, x), segment: 8 (over y, core).
Axes of the slice: x: 4, y: 4, z: 16, core: 2. Of those that a mesh axis runs over, the one named last changes fastest.
Arguments:
- block: bfloat16 [64, 4608], P('pop', 'segment'), may hold values from -6 to 6
- w_in: bfloat16 [3, 36864, 4608], P(None, 'pop', 'segment'), may hold values from -0.09375 to 0.09375
- w_out: bfloat16 [3, 36864, 4608], P(None, 'pop', 'segment'), may hold values from -0.03125 to 0.03125
- gains: float32 [3, 4608], P(None, 'segment'), may hold values from 0.5 to 1.5
- fac_left: bfloat16 [4, 4, 4, 4608], P(None, None, None, 'segment'), may hold values from -0.09375 to 0.09375
- right_perturb_factors: bfloat16 [4, 4, 4, 36864], P(None, None, None, 'pop'), may hold values from -1.796875 to 1.796875
- assign: int32 [3], replicated, may hold values from 0 to 3
Outputs:
- scores: float32 [3, 4], replicated
- final_member_activations: bfloat16 [64, 4, 4608], P('pop', None, 'segment')
The draws below stay inside these ranges and needn't reach their ends.
All inputs are finite; a program needn't handle non-finite values.
Results may differ from the reference program's by a relative error of at most 0.017.
Values may be sent and summed in bfloat16 or wider, within the bound.
No kernel may reach another device: no remote copies, remote signals or barrier semaphores. Data moves between devices by JAX's collectives and lax.ppermute only.
A program may use at most 64 MiB of HBM per device.

```python
import math
import jax
import jax.numpy as jnp
from jax import lax

D = 4608
F = 36864
MEMBERS = 4
LAYERS = 3
SECTIONS = 4
RANK = 4
TOK = 64


def level_of(rng, extent, pieces, least, largest):
    gain, own = 1.0, jax.random.fold_in(rng, 6)
    for axis_at, parts in pieces:
        steps = jnp.exp(jax.random.uniform(jax.random.fold_in(own, axis_at), (parts,), jnp.float32, least / len(pieces), largest / len(pieces)))
        gain = gain * jnp.repeat(steps, extent[axis_at] // parts).reshape([-1 if axis == axis_at else 1 for axis in range(len(extent))])
    return gain


def centred(stream_key, dims, scale, reach, shards=(), held_as=jnp.bfloat16):
    drawn = jax.random.normal(stream_key, dims, jnp.float32) * scale
    if len(shards) > 0:
        drawn = level_of(stream_key, dims, shards, -0.22, 0.18) * drawn
    return jnp.clip(drawn, min=-reach, max=reach).astype(held_as)


def setup_inputs(seed: int = 0) -> dict:
    keys = jax.random.split(jax.random.key(seed), 8)
    return {
        "block": centred(keys[0], (TOK, D), 1.0, 6.0, ((0, 64), (1, 8))),
        "w_in": centred(keys[1], (LAYERS, F, D), D ** -0.5, 0.09375, ((1, 64), (2, 8))),
        "w_out": centred(keys[2], (LAYERS, F, D), F ** -0.5, 0.03125, ((1, 64), (2, 8))),
        "gains": jnp.clip(0.5 + 1.0 * jax.random.uniform(keys[3], (LAYERS, D), jnp.float32) ** level_of(keys[3], (LAYERS, D), ((1, 8),), -0.2, 0.2), 0.5, 1.5),
        "fac_left": centred(keys[4], (MEMBERS, SECTIONS, RANK, D), D ** -0.5, 0.09375, ((3, 8),)),
        "right_perturb_factors": centred(keys[5], (MEMBERS, SECTIONS, RANK, F), 0.3, 1.796875, ((3, 64),)),
        "assign": jax.random.randint(keys[6], (LAYERS,), 0, SECTIONS).astype(jnp.int32),
    }


def normed(values):
    return values * lax.rsqrt(lax.optimization_barrier(jnp.mean(values * values, axis=-1, keepdims=True)) + 1e-06)

def reference(block, w_in, w_out, gains, fac_left, right_perturb_factors, assign):
    target = block.astype(jnp.float32)[1:]
    positions = jnp.arange(TOK - 1, dtype=jnp.float32)
    weighting = 1.0 + 2.0 * positions / (TOK - 2)
    stream = jnp.broadcast_to(block[:, None, :], (TOK, MEMBERS, D))
    per_layer = []
    for layer_pos in range(LAYERS):
        section = assign[layer_pos]
        left_fac = jnp.take(fac_left, section, axis=1).astype(jnp.float32)
        right_factor_rows = jnp.take(right_perturb_factors, section, axis=1).astype(jnp.float32)
        normal = (normed(stream.astype(jnp.float32)) * gains[layer_pos]).astype(jnp.bfloat16)
        normal32 = normal.astype(jnp.float32)
        hidden_preactivation = jnp.einsum('tmd,fd->tmf', normal32, w_in[layer_pos].astype(jnp.float32))
        reduced_dimension = jnp.einsum('tmd,mrd->tmr', normal32, left_fac)
        blended_hidden = hidden_preactivation + jnp.einsum('xwa,wan->xwn', reduced_dimension, right_factor_rows, precision=lax.Precision.HIGHEST)
        gated = jax.nn.silu(blended_hidden).astype(jnp.bfloat16)
        update = jnp.einsum('tmf,fd->tmd', gated.astype(jnp.float32), w_out[layer_pos].astype(jnp.float32))
        stream = (stream.astype(jnp.float32) + update).astype(jnp.bfloat16)
        probe = normed(stream.astype(jnp.float32))
        total = jnp.einsum('tmd,td,t->m', probe[:-1], target, weighting)
        per_layer.append(total / math.sqrt((TOK - 1) * D))
    return (jnp.stack(per_layer), stream)
```

```python
import math

import jax
import jax.numpy as jnp
from jax import lax
from jax.sharding import Mesh, PartitionSpec as P

D = 4608
BF = jnp.bfloat16
F32 = jnp.float32
SEG = ("y", "c")
EPS = 1e-06


def swap(chunks, axes):
    return lax.all_to_all(chunks, axes, 0, 0, tiled=True)


def share(value, axes, count):
    return swap(jnp.broadcast_to(value[None], (count, *value.shape)), axes)


def split_pair(value):
    high = value.astype(BF)
    low = (value - high.astype(F32)).astype(BF)
    return high, low


def dot_t(a, b, precision=None):
    return lax.dot_general(
        a, b, (((1,), (1,)), ((), ())), preferred_element_type=F32, precision=precision
    )


def packed(hidden, *extras):
    high, low = split_pair(jnp.concatenate(extras, axis=1))
    pad = 64 - 2 * high.shape[1]
    return jnp.concatenate(
        [hidden.astype(BF), high, low, jnp.zeros((hidden.shape[0], pad), BF)], axis=1
    )


def unpacked(total, width, count):
    hidden = total[:, :width]
    extras = total[:, width : width + count] + total[:, width + count : width + 2 * count]
    return hidden, extras


def local(block, w_in, w_out, gains, fac_left, right_perturb_factors, assign):
    nz, nx = lax.axis_size("z"), lax.axis_size("x")
    ns = lax.axis_size("y") * lax.axis_size("c")
    width = block.shape[1]
    hid = w_in.shape[1]
    layers = w_in.shape[0]
    members, _, rank, _ = fac_left.shape
    tok = nz * nx
    rows = tok * members
    z, x = lax.axis_index("z"), lax.axis_index("x")
    seg = lax.axis_index("y") * lax.axis_size("c") + lax.axis_index("c")

    lefts = [
        jnp.take(fac_left, assign[i], axis=1).reshape(members * rank, width) for i in range(layers)
    ]
    rights = [
        jnp.take(right_perturb_factors, assign[i], axis=1).reshape(members * rank, hid).astype(F32)
        for i in range(layers)
    ]

    base = share(block[0], ("x", "z"), tok)
    natural = jnp.swapaxes(base.reshape(nx, nz, width), 0, 1).reshape(tok, width)
    after = jnp.concatenate([natural[1:], jnp.zeros((1, width), BF)], axis=0)
    after = jnp.swapaxes(after.reshape(nz, nx, width), 0, 1).reshape(tok, width)
    place = jnp.arange(tok)
    token = (place % nz) * nx + place // nz
    weighting = jnp.where(token < tok - 1, 1.0 + 2.0 * token.astype(F32) / (tok - 2), 0.0)
    target = jnp.repeat(after, members, axis=0).astype(F32)
    row_weight = jnp.repeat(weighting, members)
    row_member = jnp.arange(rows) % members
    pick = (row_member[:, None] == (jnp.arange(members * rank) // rank)[None]).astype(F32)
    chunk = rows // ns
    own_member = jnp.arange(chunk) % members
    own_weight = lax.dynamic_slice(row_weight, (seg * chunk,), (chunk,))
    to_member = (own_member[None] == jnp.arange(members)[:, None]).astype(F32)

    my_row = x * nz + z
    mine = jnp.broadcast_to(block, (members, width))
    scores = []
    stream = None
    for layer in range(layers):
        gain = gains[layer]
        if layer == 0:
            wide = base.astype(F32)
            scaled = (wide * gain).astype(BF)
            part = packed(
                dot_t(scaled, w_in[0]),
                dot_t(scaled, lefts[0]),
                jnp.sum(wide * wide, axis=1, keepdims=True),
            )
            parts = share(part, SEG, ns).reshape(ns, tok, -1)
            total = jnp.sum(parts.astype(F32), axis=0)
            hidden, extras = unpacked(total, hid, members * rank + 1)
            scale = lax.rsqrt(extras[:, -1:] / D + EPS)
            low = extras[:, :-1].reshape(tok, members, rank)
            mixed = scale[:, None] * (
                hidden[:, None]
                + jnp.einsum(
                    "tmr,mrf->tmf",
                    low,
                    rights[0].reshape(members, rank, hid),
                    precision=lax.Precision.HIGHEST,
                )
            )
            gated = jax.nn.silu(mixed).astype(BF).reshape(rows, hid)
        else:
            wide = stream.astype(F32)
            scaled = (wide * gain).astype(BF)
            part = packed(
                dot_t(scaled, w_in[layer]),
                dot_t(scaled, lefts[layer]) * pick,
                jnp.sum(wide * wide, axis=1, keepdims=True),
                jnp.sum(wide * target, axis=1, keepdims=True),
            )
            parts = swap(part, SEG).reshape(ns, chunk, -1)
            total = jnp.sum(parts.astype(F32), axis=0)
            hidden, extras = unpacked(total, hid, members * rank + 2)
            scale = lax.rsqrt(extras[:, -2:-1] / D + EPS)
            scores.append(jnp.sum(to_member * (extras[:, -1] * scale[:, 0] * own_weight), axis=1))
            low = jnp.dot(extras[:, :-2], rights[layer], precision=lax.Precision.HIGHEST)
            gated = jax.nn.silu(scale * (hidden + low)).astype(BF)
            gated = share(gated, SEG, ns).reshape(rows, hid)
        update = jnp.dot(gated, w_out[layer], preferred_element_type=F32).astype(BF)
        part = swap(update.reshape(nx, rows // nx, width), "x")
        part = jnp.sum(part.astype(F32), axis=0).astype(BF)
        part = swap(part.reshape(nz, members, width), "z")
        mine = (mine.astype(F32) + jnp.sum(part.astype(F32), axis=0)).astype(BF)
        if layer < layers - 1:
            stream = share(mine, "z", nz).reshape(nz * members, width)
            stream = share(stream, "x", nx).reshape(rows, width)

    wide = mine.astype(F32)
    my_target = lax.dynamic_slice(after, (my_row, 0), (1, width)).astype(F32)
    first = jnp.where((z == 0) & (x == 0), 1.0, 0.0)
    sums = jnp.concatenate(
        [
            jnp.sum(wide * wide, axis=1),
            jnp.sum(wide * my_target, axis=1),
            *[first * s for s in scores],
        ]
    )
    count = nx * ns
    got = share(sums, ("x", *SEG), count).reshape(nx, ns, -1)
    got = jnp.sum(got, axis=1)
    weights_x = lax.dynamic_slice(weighting.reshape(nx, nz), (0, z), (nx, 1))
    square, along = got[:, :members], got[:, members : 2 * members]
    last = jnp.sum(along * lax.rsqrt(square / D + EPS) * weights_x, axis=0)
    earlier = jnp.sum(got[:, 2 * members :], axis=0)
    both = jnp.concatenate([earlier, last])
    both = jnp.sum(share(both, "z", nz).reshape(nz, -1), axis=0)
    return both.reshape(layers, members) / math.sqrt((tok - 1) * D), mine[None]


def solution(mesh):
    split = Mesh(mesh.devices.reshape(16, 4, 4, 2), ("z", "x", "y", "c"))
    pop = ("z", "x")
    return jax.shard_map(
        local,
        mesh=split,
        in_specs=(
            P(pop, SEG),
            P(None, pop, SEG),
            P(None, pop, SEG),
            P(None, SEG),
            P(None, None, None, SEG),
            P(None, None, None, pop),
            P(),
        ),
        out_specs=(P(), P(pop, None, SEG)),
        check_vma=False,
    )
```

```python
import math

import jax
import jax.numpy as jnp
from jax import lax
from jax.sharding import Mesh, PartitionSpec as P

D = 4608
BF = jnp.bfloat16
F32 = jnp.float32
SEG = ("y", "c")
EPS = 1e-06


def swap(chunks, axes):
    return lax.all_to_all(chunks, axes, 0, 0, tiled=True)


def share(value, axes, count):
    return swap(jnp.broadcast_to(value[None], (count, *value.shape)), axes)


def split_pair(value):
    high = value.astype(BF)
    low = (value - high.astype(F32)).astype(BF)
    return high, low


def dot_t(a, b, precision=None):
    return lax.dot_general(
        a, b, (((1,), (1,)), ((), ())), preferred_element_type=F32, precision=precision
    )


def packed(hidden, *extras):
    high, low = split_pair(jnp.concatenate(extras, axis=1))
    pad = -(hidden.shape[1] + 2 * high.shape[1]) % 128
    return jnp.concatenate(
        [hidden.astype(BF), high, low, jnp.zeros((hidden.shape[0], pad), BF)], axis=1
    )


def unpacked(total, width, count):
    hidden = total[:, :width]
    extras = total[:, width : width + count] + total[:, width + count : width + 2 * count]
    return hidden, extras


def local(block, w_in, w_out, gains, fac_left, right_perturb_factors, assign):
    nz, nx = lax.axis_size("z"), lax.axis_size("x")
    ns = lax.axis_size("y") * lax.axis_size("c")
    width = block.shape[1]
    hid = w_in.shape[1]
    layers = w_in.shape[0]
    members, _, rank, _ = fac_left.shape
    tok = nz * nx
    z, x = lax.axis_index("z"), lax.axis_index("x")
    seg = lax.axis_index("y") * lax.axis_size("c") + lax.axis_index("c")

    lefts = [
        jnp.take(fac_left, assign[i], axis=1).reshape(members * rank, width) for i in range(layers)
    ]
    near_in, near_out = [], []
    for layer in range(1, layers):
        near_in.append(lax.all_gather(w_in[layer], "x", axis=0, tiled=True))
        near_out.append(lax.all_gather(w_out[layer], "x", axis=0, tiled=True))
    rights = [
        jnp.take(right_perturb_factors, assign[i], axis=1).reshape(members * rank, hid)
        for i in range(layers)
    ]

    base = share(block[0], ("x", "z"), tok)
    natural = jnp.swapaxes(base.reshape(nx, nz, width), 0, 1).reshape(tok, width)
    after = jnp.concatenate([natural[1:], jnp.zeros((1, width), BF)], axis=0)
    near_after = lax.dynamic_slice(after.reshape(nz, nx, width), (0, x, 0), (nz, 1, width))
    near_after = near_after.reshape(nz, width)
    near_token = jnp.arange(nz) * nx + x
    near_weight = jnp.where(
        near_token < tok - 1, 1.0 + 2.0 * near_token.astype(F32) / (tok - 2), 0.0
    )
    near_rows = nz * members
    target = jnp.repeat(near_after, members, axis=0).astype(F32)
    row_weight = jnp.repeat(near_weight, members)
    row_member = jnp.arange(near_rows) % members
    pick = (row_member[:, None] == (jnp.arange(members * rank) // rank)[None]).astype(F32)
    chunk = near_rows // ns
    own_member = jnp.arange(chunk) % members
    own_weight = lax.dynamic_slice(row_weight, (seg * chunk,), (chunk,))
    to_member = (own_member[None] == jnp.arange(members)[:, None]).astype(F32)

    mine = jnp.broadcast_to(block, (members, width))
    scores = []
    stream = None
    for layer in range(layers):
        gain = gains[layer]
        if layer == 0:
            wide = base.astype(F32)
            scaled = (wide * gain).astype(BF)
            part = packed(
                dot_t(scaled, w_in[0]),
                dot_t(scaled, lefts[0]),
                jnp.sum(wide * wide, axis=1, keepdims=True),
            )
            parts = share(part, SEG, ns).reshape(ns, tok, -1)
            total = jnp.sum(parts.astype(F32), axis=0)
            hidden, extras = unpacked(total, hid, members * rank + 1)
            scale = lax.rsqrt(extras[:, -1:] / D + EPS)
            low = extras[:, :-1].reshape(tok, members, rank)
            right = rights[0].reshape(members, rank, hid).astype(F32)
            mixed = scale[:, None] * (
                hidden[:, None]
                + jnp.einsum("tmr,mrf->tmf", low, right, precision=lax.Precision.HIGHEST)
            )
            gated = jax.nn.silu(mixed).astype(BF).reshape(tok * members, hid)
            update = jnp.dot(gated, w_out[layer], preferred_element_type=F32).astype(BF)
            later = jnp.concatenate(rights[1:], axis=0)
            later = jnp.broadcast_to(later[None], (nx, *later.shape))
            part = swap(jnp.concatenate([update.reshape(nx, near_rows, width), later], axis=1), "x")
            later = jnp.swapaxes(part[:, near_rows:], 0, 1)
            later = later.reshape(layers - 1, members * rank, nx * hid).astype(F32)
            part = jnp.sum(part[:, :near_rows].astype(F32), axis=0).astype(BF)
        else:
            wide = stream.astype(F32)
            scaled = (wide * gain).astype(BF)
            part = packed(
                dot_t(scaled, near_in[layer - 1]),
                dot_t(scaled, lefts[layer]) * pick,
                jnp.sum(wide * wide, axis=1, keepdims=True),
                jnp.sum(wide * target, axis=1, keepdims=True),
            )
            parts = swap(part, SEG).reshape(ns, chunk, -1)
            total = jnp.sum(parts.astype(F32), axis=0)
            hidden, extras = unpacked(total, nx * hid, members * rank + 2)
            scale = lax.rsqrt(extras[:, -2:-1] / D + EPS)
            scores.append(
                jnp.sum(to_member * (extras[:, -1] * scale[:, 0] * own_weight), axis=1)
            )
            low = jnp.dot(extras[:, :-2], later[layer - 1], precision=lax.Precision.HIGHEST)
            gated = jax.nn.silu(scale * (hidden + low)).astype(BF)
            gated = share(gated, SEG, ns).reshape(near_rows, nx * hid)
            part = jnp.dot(gated, near_out[layer - 1], preferred_element_type=F32).astype(BF)
        part = swap(part.reshape(nz, members, width), "z")
        mine = (mine.astype(F32) + jnp.sum(part.astype(F32), axis=0)).astype(BF)
        if layer < layers - 1:
            stream = share(mine, "z", nz).reshape(near_rows, width)

    wide = mine.astype(F32)
    my_target = lax.dynamic_slice(near_after, (z, 0), (1, width)).astype(F32)
    first = jnp.where(z == 0, 1.0, 0.0)
    sums = jnp.concatenate(
        [
            jnp.sum(wide * wide, axis=1),
            jnp.sum(wide * my_target, axis=1),
            *[first * s for s in scores],
        ]
    )
    count = nx * ns
    got = share(sums, ("x", *SEG), count).reshape(nx, ns, -1)
    got = jnp.sum(got, axis=1)
    tokens = z * nx + jnp.arange(nx)
    weights = jnp.where(tokens < tok - 1, 1.0 + 2.0 * tokens.astype(F32) / (tok - 2), 0.0)
    square, along = got[:, :members], got[:, members : 2 * members]
    last = jnp.sum(along * lax.rsqrt(square / D + EPS) * weights[:, None], axis=0)
    earlier = jnp.sum(got[:, 2 * members :], axis=0)
    both = jnp.concatenate([earlier, last])
    both = jnp.sum(share(both, "z", nz).reshape(nz, -1), axis=0)
    return both.reshape(layers, members) / math.sqrt((tok - 1) * D), mine[None]


def solution(mesh):
    split = Mesh(mesh.devices.reshape(16, 4, 4, 2), ("z", "x", "y", "c"))
    pop = ("z", "x")
    return jax.shard_map(
        local,
        mesh=split,
        in_specs=(
            P(pop, SEG),
            P(None, pop, SEG),
            P(None, pop, SEG),
            P(None, SEG),
            P(None, None, None, SEG),
            P(None, None, None, pop),
            P(),
        ),
        out_specs=(P(), P(pop, None, SEG)),
        check_vma=False,
    )
```

```python
import math

import jax
import jax.numpy as jnp
from jax import lax
from jax.sharding import Mesh, PartitionSpec as P

D = 4608
BF = jnp.bfloat16
F32 = jnp.float32
SEG = ("y", "c")
EPS = 1e-06


def swap(chunks, axes):
    return lax.all_to_all(chunks, axes, 0, 0, tiled=True)


def share(value, axes, count):
    return swap(jnp.broadcast_to(value[None], (count, *value.shape)), axes)


def split_pair(value):
    high = value.astype(BF)
    low = (value - high.astype(F32)).astype(BF)
    return high, low


def dot_t(a, b, precision=None):
    return lax.dot_general(
        a, b, (((1,), (1,)), ((), ())), preferred_element_type=F32, precision=precision
    )


def packed(hidden, *extras):
    high, low = split_pair(jnp.concatenate(extras, axis=1))
    pad = -(hidden.shape[1] + 2 * high.shape[1]) % 128
    return jnp.concatenate(
        [hidden.astype(BF), high, low, jnp.zeros((hidden.shape[0], pad), BF)], axis=1
    )


def unpacked(total, width, count):
    hidden = total[:, :width]
    extras = total[:, width : width + count] + total[:, width + count : width + 2 * count]
    return hidden, extras


def local(block, w_in, w_out, gains, fac_left, right_perturb_factors, assign):
    nz, nx = lax.axis_size("z"), lax.axis_size("x")
    ny = lax.axis_size("y")
    ns = ny * lax.axis_size("c")
    width = block.shape[1]
    hid = w_in.shape[1]
    layers = w_in.shape[0]
    members, _, rank, _ = fac_left.shape
    tok = nz * nx
    z, x = lax.axis_index("z"), lax.axis_index("x")
    seg = lax.axis_index("y") * lax.axis_size("c") + lax.axis_index("c")

    lefts = [
        jnp.take(fac_left, assign[i], axis=1).reshape(members * rank, width) for i in range(layers)
    ]
    forth = [(i, (i + 1) % nx) for i in range(nx)]
    back = [(i, (i - 1) % nx) for i in range(nx)]
    flip = [(0, 1), (1, 0)]

    rights = [
        jnp.take(right_perturb_factors, assign[i], axis=1).reshape(members * rank, hid)
        for i in range(layers)
    ]

    in_far, out_far = w_in[1:], w_out[1:]
    in_left = lax.ppermute(in_far, "x", forth)
    in_right = lax.ppermute(in_far, "x", back)
    base = share(share(block, "x", nx).reshape(nx, width), "z", nz)
    natural = base.reshape(tok, width)
    base = jnp.swapaxes(base, 0, 1).reshape(tok, width)
    after = jnp.concatenate([natural[1:], jnp.zeros((1, width), BF)], axis=0)
    near_after = lax.dynamic_slice(after.reshape(nz, nx, width), (0, x, 0), (nz, 1, width))
    near_after = near_after.reshape(nz, width)
    near_token = jnp.arange(nz) * nx + x
    near_weight = jnp.where(
        near_token < tok - 1, 1.0 + 2.0 * near_token.astype(F32) / (tok - 2), 0.0
    )
    near_rows = nz * members
    target = jnp.repeat(near_after, members, axis=0).astype(F32)
    row_weight = jnp.repeat(near_weight, members)
    row_member = jnp.arange(near_rows) % members
    pick = (row_member[:, None] == (jnp.arange(members * rank) // rank)[None]).astype(F32)
    chunk = near_rows // ns
    own_member = jnp.arange(chunk) % members
    own_weight = lax.dynamic_slice(row_weight, (seg * chunk,), (chunk,))
    to_member = (own_member[None] == jnp.arange(members)[:, None]).astype(F32)

    mine = jnp.broadcast_to(block, (members, width))
    scores = []
    stream = None
    for layer in range(layers):
        gain = gains[layer]
        if layer == 0:
            wide = base.astype(F32)
            scaled = (wide * gain).astype(BF)
            part = packed(
                dot_t(scaled, w_in[0]),
                dot_t(scaled, lefts[0]),
                jnp.sum(wide * wide, axis=1, keepdims=True),
            )
            both = part.astype(F32) + lax.ppermute(part, "c", flip).astype(F32)
            part = packed(*unpacked(both, hid, members * rank + 1))
            part, in_left, in_right = lax.optimization_barrier((part, in_left, in_right))
            in_relay = lax.ppermute(in_left, "x", forth)
            parts = share(part, "y", ny)
            total = jnp.sum(parts.reshape(ny, tok, -1).astype(F32), axis=0)
            hidden, extras = unpacked(total, hid, members * rank + 1)
            scale = lax.rsqrt(extras[:, -1:] / D + EPS)
            low = extras[:, :-1].reshape(tok, members, rank)
            right = rights[0].reshape(members, rank, hid).astype(F32)
            mixed = scale[:, None] * (
                hidden[:, None]
                + jnp.einsum("tmr,mrf->tmf", low, right, precision=lax.Precision.HIGHEST)
            )
            gated = jax.nn.silu(mixed).astype(BF).reshape(tok * members, hid)
            update = jnp.dot(gated, w_out[layer], preferred_element_type=F32).astype(BF)
            sent = jnp.concatenate(rights[1:], axis=0)
            sent = jnp.broadcast_to(sent[None], (nx, *sent.shape))
            part = swap(jnp.concatenate([update.reshape(nx, near_rows, width), sent], axis=1), "x")
            late = part[:, near_rows:].astype(F32)
            late = [
                sum(late[i] * ((x + step) % nx == i).astype(F32) for i in range(nx))
                for step in (0, -1, 1, -2)
            ]
            later = jnp.concatenate(late, axis=1).reshape(layers - 1, members * rank, nx * hid)
            part = jnp.sum(part[:, :near_rows].astype(F32), axis=0).astype(BF)
            part, out_far = lax.optimization_barrier((part, out_far))
            out_left = lax.ppermute(out_far, "x", forth)
            out_right = lax.ppermute(out_far, "x", back)
        else:
            wide = stream.astype(F32)
            scaled = (wide * gain).astype(BF)
            part = packed(
                jnp.concatenate(
                    [
                        dot_t(scaled, w[layer - 1])
                        for w in (in_far, in_left, in_right, in_relay)
                    ],
                    axis=1,
                ),
                dot_t(scaled, lefts[layer]) * pick,
                jnp.sum(wide * wide, axis=1, keepdims=True),
                jnp.sum(wide * target, axis=1, keepdims=True),
            )
            parts = swap(part, SEG).reshape(ns, chunk, -1)
            total = jnp.sum(parts.astype(F32), axis=0)
            hidden, extras = unpacked(total, nx * hid, members * rank + 2)
            scale = lax.rsqrt(extras[:, -2:-1] / D + EPS)
            scores.append(
                jnp.sum(to_member * (extras[:, -1] * scale[:, 0] * own_weight), axis=1)
            )
            low = jnp.dot(extras[:, :-2], later[layer - 1], precision=lax.Precision.HIGHEST)
            gated = jax.nn.silu(scale * (hidden + low)).astype(BF)
            gated = share(gated, SEG, ns).reshape(near_rows, nx * hid)
            part = sum(
                jnp.dot(
                    gated[:, i * hid : (i + 1) * hid],
                    w[layer - 1],
                    preferred_element_type=F32,
                )
                for i, w in enumerate((out_far, out_left, out_right, out_relay))
            ).astype(BF)
        part = swap(part.reshape(nz, members, width), "z")
        mine = (mine.astype(F32) + jnp.sum(part.astype(F32), axis=0)).astype(BF)
        if layer < layers - 1:
            stream = share(mine, "z", nz).reshape(near_rows, width)
            if layer == 0:
                stream, out_left, out_right = lax.optimization_barrier(
                    (stream, out_left, out_right)
                )
                out_relay = lax.ppermute(out_left, "x", forth)

    wide = mine.astype(F32)
    my_target = lax.dynamic_slice(near_after, (z, 0), (1, width)).astype(F32)
    first = jnp.where(z == 0, 1.0, 0.0)
    sums = jnp.concatenate(
        [
            jnp.sum(wide * wide, axis=1),
            jnp.sum(wide * my_target, axis=1),
            *[first * s for s in scores],
        ]
    )
    count = nx * ns
    got = share(sums, ("x", *SEG), count).reshape(nx, ns, -1)
    got = jnp.sum(got, axis=1)
    tokens = z * nx + jnp.arange(nx)
    weights = jnp.where(tokens < tok - 1, 1.0 + 2.0 * tokens.astype(F32) / (tok - 2), 0.0)
    square, along = got[:, :members], got[:, members : 2 * members]
    last = jnp.sum(along * lax.rsqrt(square / D + EPS) * weights[:, None], axis=0)
    earlier = jnp.sum(got[:, 2 * members :], axis=0)
    both = jnp.concatenate([earlier, last])
    both = jnp.sum(share(both, "z", nz).reshape(nz, -1), axis=0)
    return both.reshape(layers, members) / math.sqrt((tok - 1) * D), mine[None]


def solution(mesh):
    split = Mesh(mesh.devices.reshape(16, 4, 4, 2), ("z", "x", "y", "c"))
    pop = ("z", "x")
    return jax.shard_map(
        local,
        mesh=split,
        in_specs=(
            P(pop, SEG),
            P(None, pop, SEG),
            P(None, pop, SEG),
            P(None, SEG),
            P(None, None, None, SEG),
            P(None, None, None, pop),
            P(),
        ),
        out_specs=(P(), P(pop, None, SEG)),
        check_vma=False,
    )
```

```python
import functools
import math

import jax
import jax.numpy as jnp
from jax import lax
from jax.experimental import pallas as pl
from jax.experimental.pallas import tpu as pltpu
from jax.sharding import Mesh, PartitionSpec as P

D = 4608
BF = jnp.bfloat16
F32 = jnp.float32
SEG = ("y", "c")
EPS = 1e-06
HALF = 64
SIDE = 128
MIB = 1 << 20


def swap(chunks, axes):
    return lax.all_to_all(chunks, axes, 0, 0, tiled=True)


def share(value, axes, count):
    return swap(jnp.broadcast_to(value[None], (count, *value.shape)), axes)


def split_pair(value):
    high = value.astype(BF)
    low = (value - high.astype(F32)).astype(BF)
    return high, low


def dot_t(a, b):
    return lax.dot_general(a, b, (((1,), (1,)), ((), ())), preferred_element_type=F32)


def packed(hidden, extras):
    high, low = split_pair(extras)
    pad = -(hidden.shape[1] + 2 * high.shape[1]) % 128
    return jnp.concatenate(
        [hidden.astype(BF), high, low, jnp.zeros((hidden.shape[0], pad), BF)], axis=1
    )


def unpacked(total, width, count):
    hidden = total[:, :width]
    extras = total[:, width : width + count] + total[:, width + count : width + 2 * count]
    return hidden, extras


def lanes(rows):
    return lax.broadcasted_iota(jnp.int32, (rows, SIDE), 1)


def fetches(parts, whole, sems):
    copies, start = [], 0
    for i, part in enumerate(parts):
        size = part.shape[0]
        copies.append(
            pltpu.make_async_copy(part, whole.at[pl.ds(start, size)], sems.at[i])
        )
        start += size
    return copies


def enter_kernel(low_lanes, stream, gain, left, target, pick, *rest):
    parts, (out, whole, sems) = rest[:-3], rest[-3:]
    copies = fetches(parts, whole, sems)
    for copy in copies:
        copy.start()
    rows = stream.shape[0]
    wide = stream[...].astype(F32)
    scaled = (wide * gain[...]).astype(BF)
    extras = dot_t(scaled, left[...]) * pick[...]
    lane = lanes(rows)
    place = lane % HALF
    square = jnp.sum(wide * wide, axis=1, keepdims=True)
    along = jnp.sum(wide * target[...].astype(F32), axis=1, keepdims=True)
    extras = jnp.where(place == low_lanes, square, extras)
    extras = jnp.where(place == low_lanes + 1, along, extras)
    high = extras.astype(BF).astype(F32)
    out[:, :SIDE] = jnp.where(lane < HALF, high, extras - high).astype(BF)
    step = 2 * whole.shape[0] // max(len(parts), 2)
    for i in range(whole.shape[0] // step):
        for copy in copies[2 * i : 2 * i + 2]:
            copy.wait()
        out[:, SIDE + i * step : SIDE + (i + 1) * step] = dot_t(
            scaled, whole[i * step : (i + 1) * step]
        ).astype(BF)


def enter(stream, gain, left, target, pick, parts, low_lanes):
    rows, width = stream.shape
    hid = sum(p.shape[0] for p in parts)
    vmem = pl.BlockSpec(memory_space=pltpu.VMEM)
    return pl.pallas_call(
        functools.partial(enter_kernel, low_lanes),
        out_shape=jax.ShapeDtypeStruct((rows, SIDE + hid), BF),
        in_specs=[vmem] * 5 + [pl.BlockSpec(memory_space=pl.ANY)] * len(parts),
        out_specs=vmem,
        scratch_shapes=[
            pltpu.VMEM((hid, width), BF),
            pltpu.SemaphoreType.DMA((len(parts),)),
        ],
        compiler_params=pltpu.CompilerParams(vmem_limit_bytes=12 * MIB),
        cost_estimate=pl.CostEstimate(
            flops=2 * rows * hid * width, bytes_accessed=2 * hid * width, transcendentals=0
        ),
        name="enter",
    )(stream, gain, left, target, pick, *parts)


def middle_kernel(low_lanes, got, right, out, side):
    count, rows, _ = got.shape
    total = got[0].astype(F32)
    for i in range(1, count):
        total += got[i].astype(F32)
    extras = total[:, :SIDE]
    place = lanes(rows) % HALF
    square = jnp.sum(jnp.where(place == low_lanes, extras, 0.0), axis=1, keepdims=True)
    along = jnp.sum(jnp.where(place == low_lanes + 1, extras, 0.0), axis=1, keepdims=True)
    scale = lax.rsqrt(square / D + EPS)
    side[...] = jnp.broadcast_to(along * scale, (rows, SIDE))
    low = jnp.zeros((rows, right.shape[1]), F32)
    left = extras
    for _ in range(3):
        piece = left.astype(BF)
        low += jnp.dot(piece, right[...], preferred_element_type=F32)
        left = left - piece.astype(F32)
    mixed = scale * (total[:, SIDE:] + low)
    gated = (mixed / (1.0 + jnp.exp(-mixed))).astype(BF)
    for i in range(count):
        out[i] = gated


def middle(got, right, low_lanes):
    count, rows, full = got.shape
    vmem = pl.BlockSpec(memory_space=pltpu.VMEM)
    return pl.pallas_call(
        functools.partial(middle_kernel, low_lanes),
        out_shape=(
            jax.ShapeDtypeStruct((count, rows, full - SIDE), BF),
            jax.ShapeDtypeStruct((rows, SIDE), F32),
        ),
        in_specs=[vmem] * 2,
        out_specs=(vmem, vmem),
        compiler_params=pltpu.CompilerParams(vmem_limit_bytes=12 * MIB),
        name="middle",
    )(got, right)


def leave_kernel(gated, *rest):
    parts, (out, whole, sems) = rest[:-3], rest[-3:]
    copies = fetches(parts, whole, sems)
    for copy in copies:
        copy.start()
    step = 2 * whole.shape[0] // max(len(parts), 2)
    total = None
    for i in range(whole.shape[0] // step):
        for copy in copies[2 * i : 2 * i + 2]:
            copy.wait()
        here = slice(i * step, (i + 1) * step)
        piece = jnp.dot(gated[:, here], whole[here], preferred_element_type=F32)
        total = piece if total is None else total + piece
    out[...] = total.astype(BF)


def leave(gated, parts):
    rows, hid = gated.shape
    width = parts[0].shape[1]
    vmem = pl.BlockSpec(memory_space=pltpu.VMEM)
    return pl.pallas_call(
        leave_kernel,
        out_shape=jax.ShapeDtypeStruct((rows, width), BF),
        in_specs=[vmem] + [pl.BlockSpec(memory_space=pl.ANY)] * len(parts),
        out_specs=vmem,
        scratch_shapes=[
            pltpu.VMEM((hid, width), BF),
            pltpu.SemaphoreType.DMA((len(parts),)),
        ],
        compiler_params=pltpu.CompilerParams(vmem_limit_bytes=12 * MIB),
        cost_estimate=pl.CostEstimate(
            flops=2 * rows * hid * width, bytes_accessed=2 * hid * width, transcendentals=0
        ),
        name="leave",
    )(gated, *parts)


def sided(factors):
    empty = jnp.zeros((HALF - factors.shape[0], factors.shape[1]), factors.dtype)
    return jnp.concatenate([factors, empty, factors, empty], axis=0)


def local(block, w_in, w_out, gains, fac_left, right_perturb_factors, assign):
    nz, nx = lax.axis_size("z"), lax.axis_size("x")
    ny = lax.axis_size("y")
    ns = ny * lax.axis_size("c")
    width = block.shape[1]
    hid = w_in.shape[1]
    layers = w_in.shape[0]
    members, _, rank, _ = fac_left.shape
    low_lanes = members * rank
    tok = nz * nx
    z, x = lax.axis_index("z"), lax.axis_index("x")
    seg = lax.axis_index("y") * lax.axis_size("c") + lax.axis_index("c")

    lefts = [
        jnp.take(fac_left, assign[i], axis=1).reshape(low_lanes, width) for i in range(layers)
    ]
    rights = [
        jnp.take(right_perturb_factors, assign[i], axis=1).reshape(low_lanes, hid)
        for i in range(layers)
    ]

    early = w_in[1]
    base = share(block.astype(F32), "x", nx).reshape(nx, width).astype(BF)
    base, far_in, far_out = lax.optimization_barrier((base, w_in, w_out))
    near_in, near_out = [], []
    for layer in range(1, layers):
        far = early if layer == 1 else far_in[layer]
        near_in.append([lax.all_gather(far, "x", axis=0, tiled=True)])
        near_out.append([lax.all_gather(far_out[layer], "x", axis=0, tiled=True)])
    base = share(base, "z", nz)
    natural = base.reshape(tok, width)
    base = jnp.swapaxes(base, 0, 1).reshape(tok, width)
    after = jnp.concatenate([natural[1:], jnp.zeros((1, width), BF)], axis=0)
    near_after = lax.dynamic_slice(after.reshape(nz, nx, width), (0, x, 0), (nz, 1, width))
    near_after = near_after.reshape(nz, width)
    near_token = jnp.arange(nz) * nx + x
    near_weight = jnp.where(
        near_token < tok - 1, 1.0 + 2.0 * near_token.astype(F32) / (tok - 2), 0.0
    )
    near_rows = nz * members
    target = jnp.repeat(near_after, members, axis=0)
    row_weight = jnp.repeat(near_weight, members)
    row_member = jnp.arange(near_rows) % members
    place = jnp.arange(SIDE) % HALF
    pick = (row_member[:, None] == (place // rank)[None]) & (place < low_lanes)[None]
    pick = pick.astype(F32)
    chunk = near_rows // ns
    own_member = jnp.arange(chunk) % members
    own_weight = lax.dynamic_slice(row_weight, (seg * chunk,), (chunk,))
    to_member = (own_member[None] == jnp.arange(members)[:, None]).astype(F32)

    mine = jnp.broadcast_to(block, (members, width))
    scores = []
    stream = None
    for layer in range(layers):
        gain = gains[layer]
        if layer == 0:
            wide = base.astype(F32)
            scaled = (wide * gain).astype(BF)
            extras = jnp.concatenate(
                [dot_t(scaled, lefts[0]), jnp.sum(wide * wide, axis=1, keepdims=True)], axis=1
            )
            part = packed(dot_t(scaled, w_in[0]), extras)
            parts = share(part, SEG, ns)
            total = jnp.sum(parts.reshape(ns, tok, -1).astype(F32), axis=0)
            hidden, extras = unpacked(total, hid, low_lanes + 1)
            scale = lax.rsqrt(extras[:, -1:] / D + EPS)
            low = extras[:, :-1].reshape(tok, members, rank)
            right = rights[0].reshape(members, rank, hid).astype(F32)
            mixed = scale[:, None] * (
                hidden[:, None]
                + jnp.einsum("tmr,mrf->tmf", low, right, precision=lax.Precision.HIGHEST)
            )
            gated = jax.nn.silu(mixed).astype(BF).reshape(tok * members, hid)
            update = jnp.dot(gated, w_out[layer], preferred_element_type=F32).astype(BF)
            sent = jnp.concatenate(rights[1:], axis=0)
            sent = jnp.broadcast_to(sent[None], (nx, *sent.shape))
            part = swap(jnp.concatenate([update.reshape(nx, near_rows, width), sent], axis=1), "x")
            late = part[:, near_rows:].astype(F32)
            late = [
                sum(late[i] * ((x + step) % nx == i).astype(F32) for i in range(nx))
                for step in (-x, 1 - x, 2 - x, 3 - x)
            ]
            later = jnp.concatenate(late, axis=1).astype(BF)
            later = [
                sided(later[i * low_lanes : (i + 1) * low_lanes]) for i in range(layers - 1)
            ]
            part = jnp.sum(part[:, :near_rows].astype(F32), axis=0).astype(BF)
        else:
            part = enter(
                stream,
                gain[None],
                sided(lefts[layer]),
                target,
                pick,
                near_in[layer - 1],
                low_lanes,
            )
            part = swap(part.reshape(ns, chunk, -1), SEG)
            gated, side = middle(part, later[layer - 1], low_lanes)
            scores.append(jnp.sum(to_member * (side[:, 0] * own_weight), axis=1))
            gated = swap(gated, SEG)
            part = leave(gated.reshape(near_rows, nx * hid), near_out[layer - 1])
        part = swap(part.reshape(nz, members, width), "z")
        mine = (mine.astype(F32) + jnp.sum(part.astype(F32), axis=0)).astype(BF)
        if layer < layers - 1:
            stream = share(mine, "z", nz)
            stream = stream.reshape(near_rows, width)

    wide = mine.astype(F32)
    my_target = lax.dynamic_slice(near_after, (z, 0), (1, width)).astype(F32)
    first = jnp.where(z == 0, 1.0, 0.0)
    sums = jnp.concatenate(
        [
            jnp.sum(wide * wide, axis=1),
            jnp.sum(wide * my_target, axis=1),
            *[first * s for s in scores],
        ]
    )
    count = nx * ns
    got = share(sums[None], ("x", *SEG), count).reshape(nx, ns, -1)
    got = jnp.sum(got, axis=1)
    tokens = z * nx + jnp.arange(nx)
    weights = jnp.where(tokens < tok - 1, 1.0 + 2.0 * tokens.astype(F32) / (tok - 2), 0.0)
    square, along = got[:, :members], got[:, members : 2 * members]
    last = jnp.sum(along * lax.rsqrt(square / D + EPS) * weights[:, None], axis=0)
    earlier = jnp.sum(got[:, 2 * members :], axis=0)
    both = jnp.concatenate([earlier, last])
    both = jnp.sum(share(both[None], "z", nz).reshape(nz, -1), axis=0)
    return both.reshape(layers, members) / math.sqrt((tok - 1) * D), mine[None]


def solution(mesh):
    split = Mesh(mesh.devices.reshape(16, 4, 4, 2), ("z", "x", "y", "c"))
    pop = ("z", "x")
    return jax.shard_map(
        local,
        mesh=split,
        in_specs=(
            P(pop, SEG),
            P(None, pop, SEG),
            P(None, pop, SEG),
            P(None, SEG),
            P(None, None, None, SEG),
            P(None, None, None, pop),
            P(),
        ),
        out_specs=(P(), P(pop, None, SEG)),
        check_vma=False,
    )
```

```python
import functools
import math

import jax
import jax.numpy as jnp
from jax import lax
from jax.experimental import pallas as pl
from jax.experimental.pallas import tpu as pltpu
from jax.sharding import Mesh, PartitionSpec as P

D = 4608
BF = jnp.bfloat16
F32 = jnp.float32
SEG = ("y", "c")
EPS = 1e-06
HALF = 64
SIDE = 128
MIB = 1 << 20
WIDE = 59 * MIB


def swap(chunks, axes):
    return lax.all_to_all(chunks, axes, 0, 0, tiled=True)


def share(value, axes, count):
    return swap(jnp.broadcast_to(value[None], (count, *value.shape)), axes)


def dot_t(a, b):
    return lax.dot_general(a, b, (((1,), (1,)), ((), ())), preferred_element_type=F32)


def lanes(rows):
    return lax.broadcasted_iota(jnp.int32, (rows, SIDE), 1)


def fetches(source, first, size, whole, sems):
    return [
        pltpu.make_async_copy(
            source.at[i, pl.ds(first, size)], whole.at[pl.ds(i * size, size)], sems.at[i]
        )
        for i in range(source.shape[0])
    ]


def side_lanes(extras, square, along, low_lanes):
    lane = lanes(extras.shape[0])
    place = lane % HALF
    extras = jnp.where(place == low_lanes, square, extras)
    if along is not None:
        extras = jnp.where(place == low_lanes + 1, along, extras)
    high = extras.astype(BF).astype(F32)
    return jnp.where(lane < HALF, high, extras - high).astype(BF)


def pack_kernel(layer, *refs):
    if len(refs) == 4:
        w_in, w_out, out, sems = refs
    else:
        w_in, w_out, block, out, copies, sems = refs
    size = w_in.shape[1]
    moves = [
        pltpu.make_async_copy(w.at[layer], out.at[pl.ds(i * size, size)], sems.at[i])
        for i, w in enumerate((w_in, w_out))
    ]
    for move in moves:
        move.start()
    if len(refs) > 4:
        copies[...] = jnp.broadcast_to(block[...][None], copies.shape)
    for move in moves:
        move.wait()


def pack(w_in, w_out, layer, block=None, count=0):
    _, size, width = w_in.shape
    hbm = pl.BlockSpec(memory_space=pltpu.HBM)
    vmem = pl.BlockSpec(memory_space=pltpu.VMEM)
    out_shape = [jax.ShapeDtypeStruct((2 * size, width), BF)]
    given = [w_in, w_out]
    if block is not None:
        given.append(block.reshape(2, width // 2))
        out_shape.append(jax.ShapeDtypeStruct((count, 2, width // 2), BF))
    got = pl.pallas_call(
        functools.partial(pack_kernel, layer),
        out_shape=out_shape,
        in_specs=[hbm] * 2 + [vmem] * (len(given) - 2),
        out_specs=[hbm] + [vmem] * (len(out_shape) - 1),
        scratch_shapes=[pltpu.SemaphoreType.DMA((2,))],
        compiler_params=pltpu.CompilerParams(vmem_limit_bytes=WIDE),
        name="pack",
    )(*given)
    return got if block is not None else got[0]


def first_kernel(low_lanes, stream, gain, left, weight, out):
    wide = stream[...].astype(F32)
    scaled = (wide * gain[...]).astype(BF)
    square = jnp.sum(wide * wide, axis=1, keepdims=True)
    extras = side_lanes(dot_t(scaled, left[...]), square, None, low_lanes)
    hidden = dot_t(scaled, weight[...]).astype(BF)
    for i in range(out.shape[0]):
        out[i, :, :SIDE] = extras
        out[i, :, SIDE:] = hidden


def first(stream, gain, left, weight, low_lanes, count):
    rows = stream.shape[0]
    hid = weight.shape[0]
    vmem = pl.BlockSpec(memory_space=pltpu.VMEM)
    return pl.pallas_call(
        functools.partial(first_kernel, low_lanes),
        out_shape=jax.ShapeDtypeStruct((count, rows, SIDE + hid), BF),
        in_specs=[vmem] * 4,
        out_specs=vmem,
        compiler_params=pltpu.CompilerParams(vmem_limit_bytes=12 * MIB),
        name="first",
    )(stream, gain, left, weight)


def enter_kernel(low_lanes, first, size, stream, gain, left, target, pick, source, out, whole, sems):
    copies = fetches(source, first, size, whole, sems)
    for copy in copies:
        copy.start()
    wide = stream[...].astype(F32)
    scaled = (wide * gain[...]).astype(BF)
    square = jnp.sum(wide * wide, axis=1, keepdims=True)
    along = jnp.sum(wide * target[...].astype(F32), axis=1, keepdims=True)
    extras = dot_t(scaled, left[...]) * pick[...]
    out[:, :SIDE] = side_lanes(extras, square, along, low_lanes)
    step = 2 * size
    for i in range(len(copies) // 2):
        copies[2 * i].wait()
        copies[2 * i + 1].wait()
        out[:, SIDE + i * step : SIDE + (i + 1) * step] = dot_t(
            scaled, whole[i * step : (i + 1) * step]
        ).astype(BF)


def enter(stream, gain, left, target, pick, source, low_lanes, first, size):
    rows, width = stream.shape
    parts = source.shape[0]
    hid = parts * size
    vmem = pl.BlockSpec(memory_space=pltpu.VMEM)
    return pl.pallas_call(
        functools.partial(enter_kernel, low_lanes, first, size),
        out_shape=jax.ShapeDtypeStruct((rows, SIDE + hid), BF),
        in_specs=[vmem] * 5 + [pl.BlockSpec(memory_space=pltpu.HBM)],
        out_specs=vmem,
        scratch_shapes=[pltpu.VMEM((hid, width), BF), pltpu.SemaphoreType.DMA((parts,))],
        compiler_params=pltpu.CompilerParams(vmem_limit_bytes=WIDE),
        cost_estimate=pl.CostEstimate(
            flops=2 * rows * hid * width, bytes_accessed=2 * hid * width, transcendentals=0
        ),
        name="enter",
    )(stream, gain, left, target, pick, source)


def middle_kernel(low_lanes, got, right, out, side):
    count, rows, _ = got.shape
    total = got[0].astype(F32)
    for i in range(1, count):
        total += got[i].astype(F32)
    extras = total[:, :SIDE]
    place = lanes(rows) % HALF
    square = jnp.sum(jnp.where(place == low_lanes, extras, 0.0), axis=1, keepdims=True)
    along = jnp.sum(jnp.where(place == low_lanes + 1, extras, 0.0), axis=1, keepdims=True)
    scale = lax.rsqrt(square / D + EPS)
    side[...] = jnp.broadcast_to(along * scale, (rows, SIDE))
    low = jnp.zeros((rows, right.shape[1]), F32)
    left = extras
    for _ in range(3):
        piece = left.astype(BF)
        low += jnp.dot(piece, right[...], preferred_element_type=F32)
        left = left - piece.astype(F32)
    mixed = scale * (total[:, SIDE:] + low)
    gated = (mixed / (1.0 + jnp.exp(-mixed))).astype(BF)
    for i in range(count):
        out[i] = gated


def middle(got, right, low_lanes):
    count, rows, full = got.shape
    vmem = pl.BlockSpec(memory_space=pltpu.VMEM)
    return pl.pallas_call(
        functools.partial(middle_kernel, low_lanes),
        out_shape=(
            jax.ShapeDtypeStruct((count, rows, full - SIDE), BF),
            jax.ShapeDtypeStruct((rows, SIDE), F32),
        ),
        in_specs=[vmem] * 2,
        out_specs=(vmem, vmem),
        compiler_params=pltpu.CompilerParams(vmem_limit_bytes=12 * MIB),
        name="middle",
    )(got, right)


def leave_kernel(first, size, gated, source, out, whole, sems):
    copies = fetches(source, first, size, whole, sems)
    for copy in copies:
        copy.start()
    step = 2 * size
    total = None
    for i in range(len(copies) // 2):
        copies[2 * i].wait()
        copies[2 * i + 1].wait()
        here = slice(i * step, (i + 1) * step)
        piece = jnp.dot(gated[:, here], whole[here], preferred_element_type=F32)
        total = piece if total is None else total + piece
    out[...] = total.astype(BF)


def leave(gated, source, first, size):
    rows, hid = gated.shape
    parts, _, width = source.shape
    vmem = pl.BlockSpec(memory_space=pltpu.VMEM)
    return pl.pallas_call(
        functools.partial(leave_kernel, first, size),
        out_shape=jax.ShapeDtypeStruct((rows, width), BF),
        in_specs=[vmem, pl.BlockSpec(memory_space=pltpu.HBM)],
        out_specs=vmem,
        scratch_shapes=[pltpu.VMEM((hid, width), BF), pltpu.SemaphoreType.DMA((parts,))],
        compiler_params=pltpu.CompilerParams(vmem_limit_bytes=WIDE),
        cost_estimate=pl.CostEstimate(
            flops=2 * rows * hid * width, bytes_accessed=2 * hid * width, transcendentals=0
        ),
        name="leave",
    )(gated, source)


def sided(factors):
    empty = jnp.zeros((HALF - factors.shape[0], factors.shape[1]), factors.dtype)
    return jnp.concatenate([factors, empty, factors, empty], axis=0)


def local(block, w_in, w_out, gains, fac_left, right_perturb_factors, assign):
    nz, nx = lax.axis_size("z"), lax.axis_size("x")
    ny = lax.axis_size("y")
    ns = ny * lax.axis_size("c")
    width = block.shape[1]
    hid = w_in.shape[1]
    layers = w_in.shape[0]
    members, _, rank, _ = fac_left.shape
    low_lanes = members * rank
    tok = nz * nx
    z, x = lax.axis_index("z"), lax.axis_index("x")
    seg = lax.axis_index("y") * lax.axis_size("c") + lax.axis_index("c")

    chosen = (jnp.arange(fac_left.shape[1])[None] == assign[:, None]).astype(F32)

    def section(factors, layer):
        picked = jnp.sum(factors.astype(F32) * chosen[layer][None, :, None, None], axis=1)
        return picked.astype(BF).reshape(low_lanes, factors.shape[-1])

    lefts = [section(fac_left, i) for i in range(layers)]
    rights = [section(right_perturb_factors, i) for i in range(layers)]
    first_right = rights[0].reshape(members, rank, hid).astype(F32)

    def gathered(packed):
        value = lax.all_gather(packed, "x", axis=0, tiled=True)
        return value.reshape(nx, 2 * hid, width)

    packed, copies = pack(w_in, w_out, 1, block, tok)
    near = [gathered(packed)]
    base = swap(copies, ("z", "x")).reshape(nz, nx, width)
    natural = base.reshape(tok, width)
    base = jnp.swapaxes(base, 0, 1).reshape(tok, width)
    after = jnp.concatenate([natural[1:], jnp.zeros((1, width), BF)], axis=0)
    near_after = lax.dynamic_slice(after.reshape(nz, nx, width), (0, x, 0), (nz, 1, width))
    near_after = near_after.reshape(nz, width)
    near_token = jnp.arange(nz) * nx + x
    near_weight = jnp.where(
        near_token < tok - 1, 1.0 + 2.0 * near_token.astype(F32) / (tok - 2), 0.0
    )
    near_rows = nz * members
    target = jnp.repeat(near_after, members, axis=0)
    row_weight = jnp.repeat(near_weight, members)
    row_member = jnp.arange(near_rows) % members
    place = jnp.arange(SIDE) % HALF
    pick = (row_member[:, None] == (place // rank)[None]) & (place < low_lanes)[None]
    pick = pick.astype(F32)
    chunk = near_rows // ns
    own_member = jnp.arange(chunk) % members
    own_weight = lax.dynamic_slice(row_weight, (seg * chunk,), (chunk,))
    to_member = (own_member[None] == jnp.arange(members)[:, None]).astype(F32)

    mine = jnp.broadcast_to(block, (members, width))
    scores = []
    stream = None
    for layer in range(layers):
        gain = gains[layer]
        if layer == 0:
            parts = first(base, gain[None], sided(lefts[0]), w_in[0], low_lanes, ns)
            parts = swap(parts, SEG)
            total = jnp.sum(parts.astype(F32), axis=0)
            extras = total[:, :HALF] + total[:, HALF:SIDE]
            scale = lax.rsqrt(extras[:, low_lanes : low_lanes + 1] / D + EPS)
            low = extras[:, :low_lanes].reshape(tok, members, rank)
            mixed = scale[:, None] * (
                total[:, None, SIDE:]
                + jnp.einsum("tmr,mrf->tmf", low, first_right, precision=lax.Precision.HIGHEST)
            )
            gated = jax.nn.silu(mixed).astype(BF).reshape(tok * members, hid)
            far_in, far_out, gated = lax.optimization_barrier((w_in, w_out, gated))
            near.append(gathered(pack(far_in, far_out, 2)))
            update = jnp.dot(gated, w_out[layer], preferred_element_type=F32).astype(BF)
            sent = jnp.concatenate(rights[1:], axis=0)
            sent = jnp.broadcast_to(sent[None], (nx, *sent.shape))
            part = swap(jnp.concatenate([update.reshape(nx, near_rows, width), sent], axis=1), "x")
            later = jnp.swapaxes(part[:, near_rows:], 0, 1).reshape(-1, nx * hid)
            later = [
                sided(later[i * low_lanes : (i + 1) * low_lanes]) for i in range(layers - 1)
            ]
            part = jnp.sum(part[:, :near_rows].astype(F32), axis=0).astype(BF)
        else:
            part = enter(
                stream,
                gain[None],
                sided(lefts[layer]),
                target,
                pick,
                near[layer - 1],
                low_lanes,
                0,
                hid,
            )
            part = swap(part.reshape(ns, chunk, -1), SEG)
            gated, side = middle(part, later[layer - 1], low_lanes)
            scores.append(jnp.sum(to_member * (side[:, 0] * own_weight), axis=1))
            gated = swap(gated, SEG)
            part = leave(
                gated.reshape(near_rows, nx * hid), near[layer - 1], hid, hid
            )
        part = swap(part.reshape(nz, members, width), "z")
        mine = (mine.astype(F32) + jnp.sum(part.astype(F32), axis=0)).astype(BF)
        if layer < layers - 1:
            stream = share(mine, "z", nz)
            stream = stream.reshape(near_rows, width)

    wide = mine.astype(F32)
    my_target = lax.dynamic_slice(near_after, (z, 0), (1, width)).astype(F32)
    once = jnp.where(z == 0, 1.0, 0.0)
    sums = jnp.concatenate(
        [
            jnp.sum(wide * wide, axis=1),
            jnp.sum(wide * my_target, axis=1),
            *[once * s for s in scores],
        ]
    )
    count = nx * ns
    got = share(sums[None], ("x", *SEG), count).reshape(nx, ns, -1)
    got = jnp.sum(got, axis=1)
    tokens = z * nx + jnp.arange(nx)
    weights = jnp.where(tokens < tok - 1, 1.0 + 2.0 * tokens.astype(F32) / (tok - 2), 0.0)
    square, along = got[:, :members], got[:, members : 2 * members]
    last = jnp.sum(along * lax.rsqrt(square / D + EPS) * weights[:, None], axis=0)
    earlier = jnp.sum(got[:, 2 * members :], axis=0)
    both = jnp.concatenate([earlier, last])
    both = jnp.sum(share(both[None], "z", nz).reshape(nz, -1), axis=0)
    return both.reshape(layers, members) / math.sqrt((tok - 1) * D), mine[None]


def solution(mesh):
    split = Mesh(mesh.devices.reshape(16, 4, 4, 2), ("z", "x", "y", "c"))
    pop = ("z", "x")
    return jax.shard_map(
        local,
        mesh=split,
        in_specs=(
            P(pop, SEG),
            P(None, pop, SEG),
            P(None, pop, SEG),
            P(None, SEG),
            P(None, None, None, SEG),
            P(None, None, None, pop),
            P(),
        ),
        out_specs=(P(), P(pop, None, SEG)),
        check_vma=False,
    )
```

```python
import functools
import math

import jax
import jax.numpy as jnp
from jax import lax
from jax.experimental import pallas as pl
from jax.experimental.pallas import tpu as pltpu
from jax.sharding import Mesh, PartitionSpec as P

D = 4608
BF = jnp.bfloat16
F32 = jnp.float32
SEG = ("y", "c")
EPS = 1e-06
HALF = 64
SIDE = 128
MIB = 1 << 20
WIDE = 59 * MIB


def swap(chunks, axes):
    return lax.all_to_all(chunks, axes, 0, 0, tiled=True)


def share(value, axes, count):
    return swap(jnp.broadcast_to(value[None], (count, *value.shape)), axes)


def dot_t(a, b):
    return lax.dot_general(a, b, (((1,), (1,)), ((), ())), preferred_element_type=F32)


def lanes(rows):
    return lax.broadcasted_iota(jnp.int32, (rows, SIDE), 1)


def side_lanes(extras, square, along, low_lanes):
    lane = lanes(extras.shape[0])
    place = lane % HALF
    extras = jnp.where(place == low_lanes, square, extras)
    if along is not None:
        extras = jnp.where(place == low_lanes + 1, along, extras)
    high = extras.astype(BF).astype(F32)
    return jnp.where(lane < HALF, high, extras - high).astype(BF)


def pack_kernel(layer, *refs):
    *given, held, sems, done = refs
    w_in, w_out = given[:2]
    out = given[-1] if len(given) == 3 else given[-2]
    size = w_in.shape[1]
    spans = [pl.ds(i * size, size) for i in range(2)]
    here = [
        pltpu.make_async_copy(w.at[layer], held.at[span], sems.at[i])
        for i, (w, span) in enumerate(zip((w_in, w_out), spans))
    ]
    there = [
        pltpu.make_async_copy(held.at[span], out.at[span], done.at[i])
        for i, span in enumerate(spans)
    ]
    for move in here:
        move.start()
    if len(given) > 3:
        block, copies = given[2], given[-1]
        half = copies.shape[2]
        wide = block[...].astype(F32)
        copies[:, 0] = jnp.broadcast_to(wide[:, :half], (copies.shape[0], half)).astype(BF)
        copies[:, 1] = jnp.broadcast_to(wide[:, half:], (copies.shape[0], half)).astype(BF)
    for move, back in zip(here, there):
        move.wait()
        back.start()
    for back in there:
        back.wait()


def pack(w_in, w_out, layer, block=None, count=0):
    _, size, width = w_in.shape
    hbm = pl.BlockSpec(memory_space=pltpu.HBM)
    vmem = pl.BlockSpec(memory_space=pltpu.VMEM)
    out_shape = [jax.ShapeDtypeStruct((2 * size, width), BF)]
    given = [w_in, w_out]
    if block is not None:
        given.append(block)
        out_shape.append(jax.ShapeDtypeStruct((count, 2, width // 2), BF))
    got = pl.pallas_call(
        functools.partial(pack_kernel, layer),
        out_shape=out_shape,
        in_specs=[hbm] * 2 + [vmem] * (len(given) - 2),
        out_specs=[hbm] + [vmem] * (len(out_shape) - 1),
        scratch_shapes=[
            pltpu.VMEM((2 * size, width), BF),
            pltpu.SemaphoreType.DMA((2,)),
            pltpu.SemaphoreType.DMA((2,)),
        ],
        compiler_params=pltpu.CompilerParams(vmem_limit_bytes=WIDE),
        name="pack",
    )(*given)
    return got if block is not None else got[0]


def first_kernel(low_lanes, stream, gain, left, weight, out):
    wide = stream[...].astype(F32)
    scaled = (wide * gain[...]).astype(BF)
    square = jnp.sum(wide * wide, axis=1, keepdims=True)
    extras = side_lanes(dot_t(scaled, left[...]), square, None, low_lanes)
    hidden = dot_t(scaled, weight[...]).astype(BF)
    for i in range(out.shape[0]):
        out[i, :, :SIDE] = extras
        out[i, :, SIDE:] = hidden


def first(stream, gain, left, weight, low_lanes, count):
    rows = stream.shape[0]
    hid = weight.shape[0]
    vmem = pl.BlockSpec(memory_space=pltpu.VMEM)
    return pl.pallas_call(
        functools.partial(first_kernel, low_lanes),
        out_shape=jax.ShapeDtypeStruct((count, rows, SIDE + hid), BF),
        in_specs=[vmem] * 4,
        out_specs=vmem,
        compiler_params=pltpu.CompilerParams(vmem_limit_bytes=12 * MIB),
        name="first",
    )(stream, gain, left, weight)


def enter_kernel(low_lanes, stream, gain, left, target, pick, weight, out):
    wide = stream[...].astype(F32)
    scaled = (wide * gain[...]).astype(BF)
    square = jnp.sum(wide * wide, axis=1, keepdims=True)
    along = jnp.sum(wide * target[...].astype(F32), axis=1, keepdims=True)
    extras = dot_t(scaled, left[...]) * pick[...]
    out[:, :SIDE] = side_lanes(extras, square, along, low_lanes)
    out[:, SIDE:] = dot_t(scaled, weight[...]).astype(BF)


def enter(stream, gain, left, target, pick, weight, low_lanes):
    rows, width = stream.shape
    hid = weight.shape[0]
    vmem = pl.BlockSpec(memory_space=pltpu.VMEM)
    return pl.pallas_call(
        functools.partial(enter_kernel, low_lanes),
        out_shape=jax.ShapeDtypeStruct((rows, SIDE + hid), BF),
        in_specs=[vmem] * 6,
        out_specs=vmem,
        compiler_params=pltpu.CompilerParams(vmem_limit_bytes=16 * MIB),
        cost_estimate=pl.CostEstimate(
            flops=2 * rows * hid * width, bytes_accessed=2 * hid * width, transcendentals=0
        ),
        name="enter",
    )(stream, gain, left, target, pick, weight)


def middle_kernel(low_lanes, got, right, out, side):
    count, rows, _ = got.shape
    total = got[0].astype(F32)
    for i in range(1, count):
        total += got[i].astype(F32)
    extras = total[:, :SIDE]
    place = lanes(rows) % HALF
    square = jnp.sum(jnp.where(place == low_lanes, extras, 0.0), axis=1, keepdims=True)
    along = jnp.sum(jnp.where(place == low_lanes + 1, extras, 0.0), axis=1, keepdims=True)
    scale = lax.rsqrt(square / D + EPS)
    side[...] = jnp.broadcast_to(along * scale, (rows, SIDE))
    low = jnp.zeros((rows, right.shape[1]), F32)
    left = extras
    for _ in range(3):
        piece = left.astype(BF)
        low += jnp.dot(piece, right[...], preferred_element_type=F32)
        left = left - piece.astype(F32)
    mixed = scale * (total[:, SIDE:] + low)
    gated = (mixed / (1.0 + jnp.exp(-mixed))).astype(BF)
    for i in range(count):
        out[i] = gated


def middle(got, right, low_lanes):
    count, rows, full = got.shape
    vmem = pl.BlockSpec(memory_space=pltpu.VMEM)
    return pl.pallas_call(
        functools.partial(middle_kernel, low_lanes),
        out_shape=(
            jax.ShapeDtypeStruct((count, rows, full - SIDE), BF),
            jax.ShapeDtypeStruct((rows, SIDE), F32),
        ),
        in_specs=[vmem] * 2,
        out_specs=(vmem, vmem),
        compiler_params=pltpu.CompilerParams(vmem_limit_bytes=12 * MIB),
        name="middle",
    )(got, right)


def leave_kernel(gated, weight, out):
    out[...] = jnp.dot(gated[...], weight[...], preferred_element_type=F32).astype(BF)


def leave(gated, weight):
    rows, hid = gated.shape
    width = weight.shape[1]
    vmem = pl.BlockSpec(memory_space=pltpu.VMEM)
    return pl.pallas_call(
        leave_kernel,
        out_shape=jax.ShapeDtypeStruct((rows, width), BF),
        in_specs=[vmem] * 2,
        out_specs=vmem,
        compiler_params=pltpu.CompilerParams(vmem_limit_bytes=16 * MIB),
        cost_estimate=pl.CostEstimate(
            flops=2 * rows * hid * width, bytes_accessed=2 * hid * width, transcendentals=0
        ),
        name="leave",
    )(gated, weight)


def sided(factors):
    empty = jnp.zeros((HALF - factors.shape[0], factors.shape[1]), factors.dtype)
    return jnp.concatenate([factors, empty, factors, empty], axis=0)


def local(block, w_in, w_out, gains, fac_left, right_perturb_factors, assign):
    nz, nx = lax.axis_size("z"), lax.axis_size("x")
    ny = lax.axis_size("y")
    ns = ny * lax.axis_size("c")
    width = block.shape[1]
    hid = w_in.shape[1]
    layers = w_in.shape[0]
    members, _, rank, _ = fac_left.shape
    low_lanes = members * rank
    tok = nz * nx
    z, x = lax.axis_index("z"), lax.axis_index("x")
    seg = lax.axis_index("y") * lax.axis_size("c") + lax.axis_index("c")

    chosen = (jnp.arange(fac_left.shape[1])[None] == assign[:, None]).astype(F32)

    def section(factors, layer):
        picked = jnp.sum(factors.astype(F32) * chosen[layer][None, :, None, None], axis=1)
        return picked.astype(BF).reshape(low_lanes, factors.shape[-1])

    lefts = [section(fac_left, i) for i in range(layers)]
    rights = [section(right_perturb_factors, i) for i in range(layers)]
    first_right = rights[0].reshape(members, rank, hid).astype(F32)

    def gathered(packed):
        value = lax.all_gather(packed, "x", axis=0, tiled=True)
        return value.reshape(nx, 2 * hid, width)

    packed, copies = pack(w_in, w_out, 1, block, tok)
    near = [gathered(packed)]
    base = swap(copies, ("z", "x")).reshape(nz, nx, width)
    natural = base.reshape(tok, width)
    base = jnp.swapaxes(base, 0, 1).reshape(tok, width)
    after = jnp.concatenate([natural[1:], jnp.zeros((1, width), BF)], axis=0)
    near_after = lax.dynamic_slice(after.reshape(nz, nx, width), (0, x, 0), (nz, 1, width))
    near_after = near_after.reshape(nz, width)
    near_token = jnp.arange(nz) * nx + x
    near_weight = jnp.where(
        near_token < tok - 1, 1.0 + 2.0 * near_token.astype(F32) / (tok - 2), 0.0
    )
    near_rows = nz * members
    target = jnp.repeat(near_after, members, axis=0)
    row_weight = jnp.repeat(near_weight, members)
    row_member = jnp.arange(near_rows) % members
    place = jnp.arange(SIDE) % HALF
    pick = (row_member[:, None] == (place // rank)[None]) & (place < low_lanes)[None]
    pick = pick.astype(F32)
    chunk = near_rows // ns
    own_member = jnp.arange(chunk) % members
    own_weight = lax.dynamic_slice(row_weight, (seg * chunk,), (chunk,))
    to_member = (own_member[None] == jnp.arange(members)[:, None]).astype(F32)

    mine = jnp.broadcast_to(block, (members, width))
    scores = []
    stream = None
    for layer in range(layers):
        gain = gains[layer]
        if layer == 0:
            parts = first(base, gain[None], sided(lefts[0]), w_in[0], low_lanes, ns)
            parts = swap(parts, SEG)
            total = jnp.sum(parts.astype(F32), axis=0)
            extras = total[:, :HALF] + total[:, HALF:SIDE]
            scale = lax.rsqrt(extras[:, low_lanes : low_lanes + 1] / D + EPS)
            low = extras[:, :low_lanes].reshape(tok, members, rank)
            mixed = scale[:, None] * (
                total[:, None, SIDE:]
                + jnp.einsum("tmr,mrf->tmf", low, first_right, precision=lax.Precision.HIGHEST)
            )
            gated = jax.nn.silu(mixed).astype(BF).reshape(tok * members, hid)
            update = jnp.dot(gated, w_out[layer], preferred_element_type=F32).astype(BF)
            sent = jnp.concatenate(rights[1:], axis=0)
            sent = jnp.broadcast_to(sent[None], (nx, *sent.shape))
            part = swap(jnp.concatenate([update.reshape(nx, near_rows, width), sent], axis=1), "x")
            later = jnp.swapaxes(part[:, near_rows:], 0, 1).reshape(-1, nx * hid)
            later = [
                sided(later[i * low_lanes : (i + 1) * low_lanes]) for i in range(layers - 1)
            ]
            part = jnp.sum(part[:, :near_rows].astype(F32), axis=0).astype(BF)
            part, far_in, far_out = lax.optimization_barrier((part, w_in, w_out))
            near.append(gathered(pack(far_in, far_out, 2)))
        else:
            part = enter(
                stream,
                gain[None],
                sided(lefts[layer]),
                target,
                pick,
                near[layer - 1][:, :hid].reshape(nx * hid, width),
                low_lanes,
            )
            part = swap(part.reshape(ns, chunk, -1), SEG)
            gated, side = middle(part, later[layer - 1], low_lanes)
            scores.append(jnp.sum(to_member * (side[:, 0] * own_weight), axis=1))
            gated = swap(gated, SEG)
            part = leave(
                gated.reshape(near_rows, nx * hid),
                near[layer - 1][:, hid:].reshape(nx * hid, width),
            )
        part = swap(part.reshape(nz, members, width), "z")
        mine = (mine.astype(F32) + jnp.sum(part.astype(F32), axis=0)).astype(BF)
        if layer < layers - 1:
            stream = share(mine, "z", nz)
            stream = stream.reshape(near_rows, width)

    wide = mine.astype(F32)
    my_target = lax.dynamic_slice(near_after, (z, 0), (1, width)).astype(F32)
    once = jnp.where(z == 0, 1.0, 0.0)
    sums = jnp.concatenate(
        [
            jnp.sum(wide * wide, axis=1),
            jnp.sum(wide * my_target, axis=1),
            *[once * s for s in scores],
        ]
    )
    count = nx * ns
    got = share(sums[None], ("x", *SEG), count).reshape(nx, ns, -1)
    got = jnp.sum(got, axis=1)
    tokens = z * nx + jnp.arange(nx)
    weights = jnp.where(tokens < tok - 1, 1.0 + 2.0 * tokens.astype(F32) / (tok - 2), 0.0)
    square, along = got[:, :members], got[:, members : 2 * members]
    last = jnp.sum(along * lax.rsqrt(square / D + EPS) * weights[:, None], axis=0)
    earlier = jnp.sum(got[:, 2 * members :], axis=0)
    both = jnp.concatenate([earlier, last])
    both = jnp.sum(share(both[None], "z", nz).reshape(nz, -1), axis=0)
    return both.reshape(layers, members) / math.sqrt((tok - 1) * D), mine[None]


def solution(mesh):
    split = Mesh(mesh.devices.reshape(16, 4, 4, 2), ("z", "x", "y", "c"))
    pop = ("z", "x")
    return jax.shard_map(
        local,
        mesh=split,
        in_specs=(
            P(pop, SEG),
            P(None, pop, SEG),
            P(None, pop, SEG),
            P(None, SEG),
            P(None, None, None, SEG),
            P(None, None, None, pop),
            P(),
        ),
        out_specs=(P(), P(pop, None, SEG)),
        check_vma=False,
    )
```

```python
import functools
import math

import jax
import jax.numpy as jnp
from jax import lax
from jax.experimental import pallas as pl
from jax.experimental.pallas import tpu as pltpu
from jax.sharding import Mesh, PartitionSpec as P

D = 4608
BF = jnp.bfloat16
F32 = jnp.float32
SEG = ("y", "c")
NEAR = ("h", "l")
FAR = "a"
DEEP = (FAR, *NEAR)
EPS = 1e-06
HALF = 64
SIDE = 128
MIB = 1 << 20
WIDE = 59 * MIB


def swap(chunks, axes):
    return lax.all_to_all(chunks, axes, 0, 0, tiled=True)


def share(value, axes, count):
    return swap(jnp.broadcast_to(value[None], (count, *value.shape)), axes)


def dot_t(a, b):
    return lax.dot_general(a, b, (((1,), (1,)), ((), ())), preferred_element_type=F32)


def lanes(rows):
    return lax.broadcasted_iota(jnp.int32, (rows, SIDE), 1)


def side_lanes(extras, square, along, low_lanes):
    lane = lanes(extras.shape[0])
    place = lane % HALF
    extras = jnp.where(place == low_lanes, square, extras)
    if along is not None:
        extras = jnp.where(place == low_lanes + 1, along, extras)
    high = extras.astype(BF).astype(F32)
    return jnp.where(lane < HALF, high, extras - high).astype(BF)


def pack_kernel(layer, *refs):
    *given, held, sems, done = refs
    w_in, w_out = given[:2]
    out = given[-1] if len(given) == 3 else given[-2]
    size = w_in.shape[1]
    spans = [pl.ds(i * size, size) for i in range(2)]
    here = [
        pltpu.make_async_copy(w.at[layer], held.at[span], sems.at[i])
        for i, (w, span) in enumerate(zip((w_in, w_out), spans))
    ]
    there = [
        pltpu.make_async_copy(held.at[span], out.at[span], done.at[i])
        for i, span in enumerate(spans)
    ]
    for move in here:
        move.start()
    if len(given) > 3:
        block, copies = given[2], given[-1]
        half = copies.shape[2]
        wide = block[...].astype(F32)
        copies[:, 0] = jnp.broadcast_to(wide[:, :half], (copies.shape[0], half)).astype(BF)
        copies[:, 1] = jnp.broadcast_to(wide[:, half:], (copies.shape[0], half)).astype(BF)
    for move, back in zip(here, there):
        move.wait()
        back.start()
    for back in there:
        back.wait()


def pack(w_in, w_out, layer, block=None, count=0):
    _, size, width = w_in.shape
    hbm = pl.BlockSpec(memory_space=pltpu.HBM)
    vmem = pl.BlockSpec(memory_space=pltpu.VMEM)
    out_shape = [jax.ShapeDtypeStruct((2 * size, width), BF)]
    given = [w_in, w_out]
    if block is not None:
        given.append(block)
        out_shape.append(jax.ShapeDtypeStruct((count, 2, width // 2), BF))
    got = pl.pallas_call(
        functools.partial(pack_kernel, layer),
        out_shape=out_shape,
        in_specs=[hbm] * 2 + [vmem] * (len(given) - 2),
        out_specs=[hbm] + [vmem] * (len(out_shape) - 1),
        scratch_shapes=[
            pltpu.VMEM((2 * size, width), BF),
            pltpu.SemaphoreType.DMA((2,)),
            pltpu.SemaphoreType.DMA((2,)),
        ],
        compiler_params=pltpu.CompilerParams(vmem_limit_bytes=WIDE),
        name="pack",
    )(*given)
    return got if block is not None else got[0]


def first_kernel(low_lanes, stream, gain, left, weight, out):
    wide = stream[...].astype(F32)
    scaled = (wide * gain[...]).astype(BF)
    square = jnp.sum(wide * wide, axis=1, keepdims=True)
    extras = side_lanes(dot_t(scaled, left[...]), square, None, low_lanes)
    hidden = dot_t(scaled, weight[...]).astype(BF)
    for i in range(out.shape[0]):
        out[i, :, :SIDE] = extras
        out[i, :, SIDE:] = hidden


def first(stream, gain, left, weight, low_lanes, count):
    rows = stream.shape[0]
    hid = weight.shape[0]
    vmem = pl.BlockSpec(memory_space=pltpu.VMEM)
    return pl.pallas_call(
        functools.partial(first_kernel, low_lanes),
        out_shape=jax.ShapeDtypeStruct((count, rows, SIDE + hid), BF),
        in_specs=[vmem] * 4,
        out_specs=vmem,
        compiler_params=pltpu.CompilerParams(vmem_limit_bytes=12 * MIB),
        name="first",
    )(stream, gain, left, weight)


def summed(parts):
    total = parts[0].astype(F32)
    for i in range(1, parts.shape[0]):
        total += parts[i].astype(F32)
    return total


def fold_kernel(rows, parts, out):
    total = parts[0, :rows].astype(F32)
    for i in range(1, parts.shape[0]):
        total += parts[i, :rows].astype(F32)
    total = total.astype(BF)
    for i in range(out.shape[0]):
        out[i] = total


def fold(parts, count, rows):
    vmem = pl.BlockSpec(memory_space=pltpu.VMEM)
    return pl.pallas_call(
        functools.partial(fold_kernel, rows),
        out_shape=jax.ShapeDtypeStruct((count, rows, parts.shape[2]), BF),
        in_specs=[vmem],
        out_specs=vmem,
        compiler_params=pltpu.CompilerParams(vmem_limit_bytes=8 * MIB),
        name="fold",
    )(parts)


def enter_kernel(low_lanes, parts, before, gain, left, target, pick, weight, out, stream):
    fresh = (before[...].astype(F32) + summed(parts)).astype(BF)
    stream[...] = fresh
    wide = fresh.astype(F32)
    scaled = (wide * gain[...]).astype(BF)
    square = jnp.sum(wide * wide, axis=1, keepdims=True)
    along = jnp.sum(wide * target[...].astype(F32), axis=1, keepdims=True)
    extras = dot_t(scaled, left[...]) * pick[...]
    out[:, :SIDE] = side_lanes(extras, square, along, low_lanes)
    out[:, SIDE:] = dot_t(scaled, weight[...]).astype(BF)


def enter(parts, before, gain, left, target, pick, weight, low_lanes):
    rows, width = before.shape
    hid = weight.shape[0]
    vmem = pl.BlockSpec(memory_space=pltpu.VMEM)
    return pl.pallas_call(
        functools.partial(enter_kernel, low_lanes),
        out_shape=(
            jax.ShapeDtypeStruct((rows, SIDE + hid), BF),
            jax.ShapeDtypeStruct((rows, width), BF),
        ),
        in_specs=[vmem] * 7,
        out_specs=(vmem, vmem),
        compiler_params=pltpu.CompilerParams(vmem_limit_bytes=16 * MIB),
        cost_estimate=pl.CostEstimate(
            flops=2 * rows * hid * width, bytes_accessed=2 * hid * width, transcendentals=0
        ),
        name="enter",
    )(parts, before, gain, left, target, pick, weight)


def last_kernel(parts, before, target, out, sides):
    fresh = (before[...].astype(F32) + summed(parts)).astype(BF)
    out[...] = fresh
    wide = fresh.astype(F32)
    square = jnp.sum(wide * wide, axis=1, keepdims=True)
    along = jnp.sum(wide * target[...].astype(F32), axis=1, keepdims=True)
    sides[...] = jnp.where(lanes(fresh.shape[0]) < HALF, square, along)


def last(parts, before, target):
    rows, width = before.shape
    vmem = pl.BlockSpec(memory_space=pltpu.VMEM)
    return pl.pallas_call(
        last_kernel,
        out_shape=(
            jax.ShapeDtypeStruct((rows, width), BF),
            jax.ShapeDtypeStruct((rows, SIDE), F32),
        ),
        in_specs=[vmem] * 3,
        out_specs=(vmem, vmem),
        compiler_params=pltpu.CompilerParams(vmem_limit_bytes=8 * MIB),
        name="last",
    )(parts, before, target)


def middle_kernel(low_lanes, got, right, out, side):
    count, rows, _ = got.shape
    total = got[0].astype(F32)
    for i in range(1, count):
        total += got[i].astype(F32)
    extras = total[:, :SIDE]
    place = lanes(rows) % HALF
    square = jnp.sum(jnp.where(place == low_lanes, extras, 0.0), axis=1, keepdims=True)
    along = jnp.sum(jnp.where(place == low_lanes + 1, extras, 0.0), axis=1, keepdims=True)
    scale = lax.rsqrt(square / D + EPS)
    side[...] = jnp.broadcast_to(along * scale, (rows, SIDE))
    low = jnp.zeros((rows, right.shape[1]), F32)
    left = extras
    for _ in range(3):
        piece = left.astype(BF)
        low += jnp.dot(piece, right[...], preferred_element_type=F32)
        left = left - piece.astype(F32)
    mixed = scale * (total[:, SIDE:] + low)
    gated = (mixed / (1.0 + jnp.exp(-mixed))).astype(BF)
    for i in range(count):
        out[i] = gated


def middle(got, right, low_lanes):
    count, rows, full = got.shape
    vmem = pl.BlockSpec(memory_space=pltpu.VMEM)
    return pl.pallas_call(
        functools.partial(middle_kernel, low_lanes),
        out_shape=(
            jax.ShapeDtypeStruct((count, rows, full - SIDE), BF),
            jax.ShapeDtypeStruct((rows, SIDE), F32),
        ),
        in_specs=[vmem] * 2,
        out_specs=(vmem, vmem),
        compiler_params=pltpu.CompilerParams(vmem_limit_bytes=12 * MIB),
        name="middle",
    )(got, right)


def leave_kernel(gated, weight, out):
    part = jnp.dot(gated[...], weight[...], preferred_element_type=F32).astype(BF)
    for i in range(out.shape[0]):
        out[i] = part


def leave(gated, weight, count):
    rows, hid = gated.shape
    width = weight.shape[1]
    vmem = pl.BlockSpec(memory_space=pltpu.VMEM)
    return pl.pallas_call(
        leave_kernel,
        out_shape=jax.ShapeDtypeStruct((count, rows, width), BF),
        in_specs=[vmem] * 2,
        out_specs=vmem,
        compiler_params=pltpu.CompilerParams(vmem_limit_bytes=16 * MIB),
        cost_estimate=pl.CostEstimate(
            flops=2 * rows * hid * width, bytes_accessed=2 * hid * width, transcendentals=0
        ),
        name="leave",
    )(gated, weight)


def sided(factors):
    empty = jnp.zeros((HALF - factors.shape[0], factors.shape[1]), factors.dtype)
    return jnp.concatenate([factors, empty, factors, empty], axis=0)


def local(block, w_in, w_out, gains, fac_left, right_perturb_factors, assign):
    nz, nx = lax.axis_size(DEEP), lax.axis_size("x")
    nf, nn = lax.axis_size(FAR), lax.axis_size(NEAR)
    ny = lax.axis_size("y")
    ns = ny * lax.axis_size("c")
    width = block.shape[1]
    hid = w_in.shape[1]
    layers = w_in.shape[0]
    members, _, rank, _ = fac_left.shape
    low_lanes = members * rank
    tok = nz * nx
    z, x = lax.axis_index(DEEP), lax.axis_index("x")
    seg = lax.axis_index("y") * lax.axis_size("c") + lax.axis_index("c")

    chosen = (jnp.arange(fac_left.shape[1])[None] == assign[:, None]).astype(F32)

    def section(factors, layer):
        picked = jnp.sum(factors.astype(F32) * chosen[layer][None, :, None, None], axis=1)
        return picked.astype(BF).reshape(low_lanes, factors.shape[-1])

    lefts = [section(fac_left, i) for i in range(layers)]
    rights = [section(right_perturb_factors, i) for i in range(layers)]
    first_right = rights[0].reshape(members, rank, hid).astype(F32)

    def gathered(packed):
        value = lax.all_gather(packed, "x", axis=0, tiled=True)
        return value.reshape(nx, 2 * hid, width)

    packed, copies = pack(w_in, w_out, 1, block, tok)
    near = [gathered(packed)]
    base = swap(copies, (*DEEP, "x")).reshape(nz, nx, width)
    natural = base.reshape(tok, width)
    near_base = lax.dynamic_slice(base, (0, x, 0), (nz, 1, width))
    stream = jnp.repeat(near_base.reshape(nz, width), members, axis=0)
    base = jnp.swapaxes(base, 0, 1).reshape(tok, width)
    after = jnp.concatenate([natural[1:], jnp.zeros((1, width), BF)], axis=0)
    near_after = lax.dynamic_slice(after.reshape(nz, nx, width), (0, x, 0), (nz, 1, width))
    near_after = near_after.reshape(nz, width)
    near_token = jnp.arange(nz) * nx + x
    near_weight = jnp.where(
        near_token < tok - 1, 1.0 + 2.0 * near_token.astype(F32) / (tok - 2), 0.0
    )
    near_rows = nz * members
    target = jnp.repeat(near_after, members, axis=0)
    row_weight = jnp.repeat(near_weight, members)
    row_member = jnp.arange(near_rows) % members
    place = jnp.arange(SIDE) % HALF
    pick = (row_member[:, None] == (place // rank)[None]) & (place < low_lanes)[None]
    pick = pick.astype(F32)
    chunk = near_rows // ns
    own_member = jnp.arange(chunk) % members
    own_weight = lax.dynamic_slice(row_weight, (seg * chunk,), (chunk,))
    to_member = (own_member[None] == jnp.arange(members)[:, None]).astype(F32)

    scores = []
    parts = None
    for layer in range(layers):
        gain = gains[layer]
        if layer == 0:
            parts = first(base, gain[None], sided(lefts[0]), w_in[0], low_lanes, ns)
            parts = swap(parts, SEG)
            total = jnp.sum(parts.astype(F32), axis=0)
            extras = total[:, :HALF] + total[:, HALF:SIDE]
            scale = lax.rsqrt(extras[:, low_lanes : low_lanes + 1] / D + EPS)
            low = extras[:, :low_lanes].reshape(tok, members, rank)
            mixed = scale[:, None] * (
                total[:, None, SIDE:]
                + jnp.einsum("tmr,mrf->tmf", low, first_right, precision=lax.Precision.HIGHEST)
            )
            gated = jax.nn.silu(mixed).astype(BF).reshape(tok * members, hid)
            update = jnp.dot(gated, w_out[layer], preferred_element_type=F32).astype(BF)
            sent = jnp.concatenate(rights[1:], axis=0)
            sent = jnp.broadcast_to(sent[None], (nx, *sent.shape))
            part = swap(jnp.concatenate([update.reshape(nx, near_rows, width), sent], axis=1), "x")
            later = jnp.swapaxes(part[:, near_rows:], 0, 1).reshape(-1, nx * hid)
            later = [
                sided(later[i * low_lanes : (i + 1) * low_lanes]) for i in range(layers - 1)
            ]
            part = fold(part, nn, near_rows)
            part, far_in, far_out = lax.optimization_barrier((part, w_in, w_out))
            near.append(gathered(pack(far_in, far_out, 2)))
        else:
            part, stream = enter(
                parts,
                stream,
                gain[None],
                sided(lefts[layer]),
                target,
                pick,
                weight_in,
                low_lanes,
            )
            part = swap(part.reshape(ns, chunk, -1), SEG)
            gated, side = middle(part, later[layer - 1], low_lanes)
            scores.append(jnp.sum(to_member * (side[:, 0] * own_weight), axis=1))
            gated, weight_out = lax.optimization_barrier(
                (swap(gated, SEG), near[layer - 1][:, hid:].reshape(nx * hid, width))
            )
            part = leave(gated.reshape(near_rows, nx * hid), weight_out, nn)
        parts = swap(fold(swap(part, NEAR), nf, near_rows), FAR)
        if layer < layers - 1:
            parts, weight_in = lax.optimization_barrier(
                (parts, near[layer][:, :hid].reshape(nx * hid, width))
            )

    final, sides = last(parts, stream, target)
    sums = jnp.concatenate([sides[:, 0], sides[:, HALF], *scores])
    count = nx * ns
    got = share(sums[None], ("x", *SEG), count).reshape(nx, ns, -1)
    got = jnp.sum(got, axis=1)
    square, along = got[:, :near_rows], got[:, near_rows : 2 * near_rows]
    tokens = (jnp.arange(near_rows) // members)[None] * nx + jnp.arange(nx)[:, None]
    weights = jnp.where(tokens < tok - 1, 1.0 + 2.0 * tokens.astype(F32) / (tok - 2), 0.0)
    each = along * lax.rsqrt(square / D + EPS) * weights
    latest = jnp.sum(each.reshape(nx * nz, members), axis=0)
    earlier = jnp.sum(got[:, 2 * near_rows :], axis=0)
    both = jnp.concatenate([earlier, latest])
    mine = lax.dynamic_slice(final.reshape(nz, members, width), (z, 0, 0), (1, members, width))
    return both.reshape(layers, members) / math.sqrt((tok - 1) * D), mine


def solution(mesh):
    split = Mesh(mesh.devices.reshape(4, 2, 2, 4, 4, 2), (*DEEP, "x", *SEG))
    pop = (*DEEP, "x")
    return jax.shard_map(
        local,
        mesh=split,
        in_specs=(
            P(pop, SEG),
            P(None, pop, SEG),
            P(None, pop, SEG),
            P(None, SEG),
            P(None, None, None, SEG),
            P(None, None, None, pop),
            P(),
        ),
        out_specs=(P(), P(pop, None, SEG)),
        check_vma=False,
    )
```

```python
import math

import jax
import jax.numpy as jnp
from jax import lax
from jax.sharding import Mesh, PartitionSpec as P

D = 4608
BF = jnp.bfloat16
F32 = jnp.float32
SEG = ("y", "c")
FAR = "a"
NEAR = ("h", "l", "x")
DEEP = ("h", "l", FAR)
EPS = 1e-06


def swap(chunks, axes):
    return lax.all_to_all(chunks, axes, 0, 0, tiled=True)


def share(value, axes, count):
    return swap(jnp.broadcast_to(value[None], (count, *value.shape)), axes)


def split_pair(value):
    high = value.astype(BF)
    low = (value - high.astype(F32)).astype(BF)
    return high, low


def dot_t(a, b, precision=None):
    return lax.dot_general(
        a, b, (((1,), (1,)), ((), ())), preferred_element_type=F32, precision=precision
    )


def packed(hidden, *extras):
    high, low = split_pair(jnp.concatenate(extras, axis=1))
    pad = 64 - 2 * high.shape[1]
    return jnp.concatenate(
        [hidden.astype(BF), high, low, jnp.zeros((hidden.shape[0], pad), BF)], axis=1
    )


def unpacked(total, width, count):
    hidden = total[:, :width]
    extras = total[:, width : width + count] + total[:, width + count : width + 2 * count]
    return hidden, extras


def local(block, w_in, w_out, gains, fac_left, right_perturb_factors, assign):
    nf, nn = lax.axis_size(FAR), lax.axis_size(NEAR)
    nx, nz = lax.axis_size("x"), lax.axis_size(DEEP)
    ns = lax.axis_size("y") * lax.axis_size("c")
    width = block.shape[1]
    hid = w_in.shape[1]
    layers = w_in.shape[0]
    members, _, rank, _ = fac_left.shape
    tok = nf * nn
    rows = tok * members
    far, near = lax.axis_index(FAR), lax.axis_index(NEAR)
    seg = lax.axis_index("y") * lax.axis_size("c") + lax.axis_index("c")

    lefts = [
        jnp.take(fac_left, assign[i], axis=1).reshape(members * rank, width) for i in range(layers)
    ]
    rights = [
        jnp.take(right_perturb_factors, assign[i], axis=1).reshape(members * rank, hid).astype(F32)
        for i in range(layers)
    ]

    base = share(block[0], (*NEAR, FAR), tok)
    natural = jnp.swapaxes(base.reshape(nn, nf, width), 0, 1).reshape(tok, width)
    after = jnp.concatenate([natural[1:], jnp.zeros((1, width), BF)], axis=0)
    after = jnp.swapaxes(after.reshape(nf, nn, width), 0, 1).reshape(tok, width)
    place = jnp.arange(tok)
    token = (place % nf) * nn + place // nf
    weighting = jnp.where(token < tok - 1, 1.0 + 2.0 * token.astype(F32) / (tok - 2), 0.0)
    target = jnp.repeat(after, members, axis=0).astype(F32)
    row_weight = jnp.repeat(weighting, members)
    row_member = jnp.arange(rows) % members
    pick = (row_member[:, None] == (jnp.arange(members * rank) // rank)[None]).astype(F32)
    chunk = rows // ns
    own_member = jnp.arange(chunk) % members
    own_weight = lax.dynamic_slice(row_weight, (seg * chunk,), (chunk,))
    to_member = (own_member[None] == jnp.arange(members)[:, None]).astype(F32)

    group = nf * members
    my_row = near * nf + far
    scores = []
    stream = jnp.repeat(base, members, axis=0)
    for layer in range(layers):
        gain = gains[layer]
        if layer == 0:
            wide = base.astype(F32)
            scaled = (wide * gain).astype(BF)
            part = packed(
                dot_t(scaled, w_in[0]),
                dot_t(scaled, lefts[0]),
                jnp.sum(wide * wide, axis=1, keepdims=True),
            )
            parts = share(part, SEG, ns).reshape(ns, tok, -1)
            total = jnp.sum(parts.astype(F32), axis=0)
            hidden, extras = unpacked(total, hid, members * rank + 1)
            scale = lax.rsqrt(extras[:, -1:] / D + EPS)
            low = extras[:, :-1].reshape(tok, members, rank)
            mixed = scale[:, None] * (
                hidden[:, None]
                + jnp.einsum(
                    "tmr,mrf->tmf",
                    low,
                    rights[0].reshape(members, rank, hid),
                    precision=lax.Precision.HIGHEST,
                )
            )
            gated = jax.nn.silu(mixed).astype(BF).reshape(rows, hid)
        else:
            wide = stream.astype(F32)
            scaled = (wide * gain).astype(BF)
            part = packed(
                dot_t(scaled, w_in[layer]),
                dot_t(scaled, lefts[layer]) * pick,
                jnp.sum(wide * wide, axis=1, keepdims=True),
                jnp.sum(wide * target, axis=1, keepdims=True),
            )
            parts = swap(part, SEG).reshape(ns, chunk, -1)
            total = jnp.sum(parts.astype(F32), axis=0)
            hidden, extras = unpacked(total, hid, members * rank + 2)
            scale = lax.rsqrt(extras[:, -2:-1] / D + EPS)
            scores.append(jnp.sum(to_member * (extras[:, -1] * scale[:, 0] * own_weight), axis=1))
            low = jnp.dot(extras[:, :-2], rights[layer], precision=lax.Precision.HIGHEST)
            gated = jax.nn.silu(scale * (hidden + low)).astype(BF)
            gated = share(gated, SEG, ns).reshape(rows, hid)
        update = jnp.dot(gated, w_out[layer], preferred_element_type=F32).astype(BF)
        if layer < layers - 1:
            part = swap(update.reshape(nn, group, width), NEAR)
            part = jnp.sum(part.astype(F32), axis=0).astype(BF)
            parts = share(part, FAR, nf).reshape(nf, group, width)
            held = lax.dynamic_slice(stream, (near * group, 0), (group, width))
            fresh = (held.astype(F32) + jnp.sum(parts.astype(F32), axis=0)).astype(BF)
            stream = share(fresh, NEAR, nn).reshape(rows, width)
        else:
            part = jnp.swapaxes(update.reshape(nn // nx, nx, group, width), 0, 1)
            part = swap(part.reshape(nx, rows // nx, width), "x")
            part = jnp.sum(part.astype(F32), axis=0).astype(BF)
            part = swap(part.reshape(nz, members, width), DEEP)
            held = lax.dynamic_slice(stream, (my_row * members, 0), (members, width))
            mine = (held.astype(F32) + jnp.sum(part.astype(F32), axis=0)).astype(BF)

    wide = mine.astype(F32)
    my_target = lax.dynamic_slice(after, (my_row, 0), (1, width)).astype(F32)
    first = jnp.where(my_row == 0, 1.0, 0.0)
    sums = jnp.concatenate(
        [
            jnp.sum(wide * wide, axis=1),
            jnp.sum(wide * my_target, axis=1),
            *[first * s for s in scores],
        ]
    )
    count = nx * ns
    got = share(sums, ("x", *SEG), count).reshape(nx, ns, -1)
    got = jnp.sum(got, axis=1)
    tokens = far * nn + (near // nx) * nx + jnp.arange(nx)
    weights_x = jnp.where(tokens < tok - 1, 1.0 + 2.0 * tokens.astype(F32) / (tok - 2), 0.0)
    weights_x = weights_x[:, None]
    square, along = got[:, :members], got[:, members : 2 * members]
    last = jnp.sum(along * lax.rsqrt(square / D + EPS) * weights_x, axis=0)
    earlier = jnp.sum(got[:, 2 * members :], axis=0)
    both = jnp.concatenate([earlier, last])
    both = jnp.sum(share(both, DEEP, nz).reshape(nz, -1), axis=0)
    return both.reshape(layers, members) / math.sqrt((tok - 1) * D), mine[None]


def solution(mesh):
    split = Mesh(mesh.devices.reshape(4, 2, 2, 4, 4, 2), (FAR, *NEAR, *SEG))
    pop = (FAR, *NEAR)
    return jax.shard_map(
        local,
        mesh=split,
        in_specs=(
            P(pop, SEG),
            P(None, pop, SEG),
            P(None, pop, SEG),
            P(None, SEG),
            P(None, None, None, SEG),
            P(None, None, None, pop),
            P(),
        ),
        out_specs=(P(), P(pop, None, SEG)),
        check_vma=False,
    )
```

```python
import functools
import math

import jax
import jax.numpy as jnp
from jax import lax
from jax.experimental import pallas as pl
from jax.experimental.pallas import tpu as pltpu
from jax.sharding import Mesh, PartitionSpec as P

D = 4608
BF = jnp.bfloat16
F32 = jnp.float32
SEG = ("y", "c")
FAR = "a"
NEAR = ("h", "l", "x")
EPS = 1e-06
HALF = 32
SIDE = 2 * HALF
TILE = 128
MIB = 1 << 20


def swap(chunks, axes):
    return lax.all_to_all(chunks, axes, 0, 0, tiled=True)


def share(value, axes, count):
    return swap(jnp.broadcast_to(value[None], (count, *value.shape)), axes)


def dot_t(a, b):
    return lax.dot_general(a, b, (((1,), (1,)), ((), ())), preferred_element_type=F32)


def kernel_call(body, out_shape, name, *given):
    vmem = pl.BlockSpec(memory_space=pltpu.VMEM)
    return pl.pallas_call(
        body,
        out_shape=out_shape,
        in_specs=[vmem] * len(given),
        out_specs=jax.tree.map(lambda _: vmem, out_shape),
        compiler_params=pltpu.CompilerParams(vmem_limit_bytes=12 * MIB),
        name=name,
    )(*given)


def with_sides(full, square, along, pick, low_lanes):
    tile = full[:, :TILE]
    lane = lax.broadcasted_iota(jnp.int32, tile.shape, 1)
    place = lane % HALF
    sides = tile if pick is None else tile * pick
    sides = jnp.where(place == low_lanes, square, sides)
    if along is not None:
        sides = jnp.where(place == low_lanes + 1, along, sides)
    high = sides.astype(BF).astype(F32)
    sides = jnp.where(lane < HALF, high, sides - high)
    return jnp.where(lane < SIDE, sides, tile).astype(BF)


def first_kernel(low_lanes, stream, gain, weight, out):
    wide = stream[...].astype(F32)
    full = dot_t((wide * gain[...]).astype(BF), weight[...])
    square = jnp.sum(wide * wide, axis=1, keepdims=True)
    tile = with_sides(full, square, None, None, low_lanes)
    rest = full[:, TILE:].astype(BF)
    for i in range(out.shape[0]):
        out[i, :, :TILE] = tile
        out[i, :, TILE:] = rest


def first(stream, gain, weight, low_lanes, count):
    shape = jax.ShapeDtypeStruct((count, stream.shape[0], weight.shape[0]), BF)
    return kernel_call(
        functools.partial(first_kernel, low_lanes), shape, "first", stream, gain, weight
    )


def enter_kernel(low_lanes, stream, gain, target, pick, weight, out):
    wide = stream[...].astype(F32)
    full = dot_t((wide * gain[...]).astype(BF), weight[...])
    square = jnp.sum(wide * wide, axis=1, keepdims=True)
    along = jnp.sum(wide * target[...].astype(F32), axis=1, keepdims=True)
    out[:, :TILE] = with_sides(full, square, along, pick[...], low_lanes)
    out[:, TILE:] = full[:, TILE:].astype(BF)


def enter(stream, gain, target, pick, weight, low_lanes):
    shape = jax.ShapeDtypeStruct((stream.shape[0], weight.shape[0]), BF)
    return kernel_call(
        functools.partial(enter_kernel, low_lanes),
        shape,
        "enter",
        stream,
        gain,
        target,
        pick,
        weight,
    )


def middle_kernel(low_lanes, got, right, out, side):
    total = got[0].astype(F32)
    for i in range(1, got.shape[0]):
        total += got[i].astype(F32)
    extras = total[:, :TILE]
    lane = lax.broadcasted_iota(jnp.int32, extras.shape, 1)
    extras = jnp.where(lane < SIDE, extras, 0.0)
    place = lane % HALF
    square = jnp.sum(jnp.where(place == low_lanes, extras, 0.0), axis=1, keepdims=True)
    along = jnp.sum(jnp.where(place == low_lanes + 1, extras, 0.0), axis=1, keepdims=True)
    scale = lax.rsqrt(square / D + EPS)
    side[...] = jnp.broadcast_to(along * scale, side.shape)
    low = jnp.zeros(total.shape, F32)
    left = extras
    for _ in range(3):
        piece = left.astype(BF)
        low += jnp.dot(piece, right[...], preferred_element_type=F32)
        left = left - piece.astype(F32)
    mixed = scale * (total + low)
    gated = mixed / (1.0 + jnp.exp(-mixed))
    tile = jnp.where(lane < SIDE, 0.0, gated[:, :TILE]).astype(BF)
    rest = gated[:, TILE:].astype(BF)
    for i in range(out.shape[0]):
        out[i, :, :TILE] = tile
        out[i, :, TILE:] = rest


def middle(got, right, low_lanes):
    shapes = (
        jax.ShapeDtypeStruct(got.shape, BF),
        jax.ShapeDtypeStruct((got.shape[1], TILE), F32),
    )
    return kernel_call(functools.partial(middle_kernel, low_lanes), shapes, "middle", got, right)


def leave_kernel(gated, weight, out):
    out[...] = jnp.dot(gated[...], weight[...], preferred_element_type=F32).astype(BF)


def leave(gated, weight):
    shape = jax.ShapeDtypeStruct((gated.shape[0], weight.shape[1]), BF)
    return kernel_call(leave_kernel, shape, "leave", gated, weight)


def twice(factors):
    return jnp.pad(
        jnp.concatenate([jnp.pad(factors, ((0, HALF - factors.shape[0]), (0, 0))), factors]),
        ((0, HALF - factors.shape[0]), (0, 0)),
    )


def local(block, w_in, w_out, gains, fac_left, right_perturb_factors, assign):
    nf, nn = lax.axis_size(FAR), lax.axis_size(NEAR)
    nx = lax.axis_size("x")
    ns = lax.axis_size("y") * lax.axis_size("c")
    width = block.shape[1]
    hid = w_in.shape[1]
    layers = w_in.shape[0]
    members, _, rank, _ = fac_left.shape
    tok = nf * nn
    rows = tok * members
    far, near = lax.axis_index(FAR), lax.axis_index(NEAR)
    seg = lax.axis_index("y") * lax.axis_size("c") + lax.axis_index("c")

    low_lanes = members * rank
    chosen = (jnp.arange(fac_left.shape[1])[None] == assign[:, None]).astype(F32)

    def section(factors, layer):
        picked = jnp.sum(factors.astype(F32) * chosen[layer][None, :, None, None], axis=1)
        return picked.astype(BF).reshape(low_lanes, factors.shape[-1])

    stacked_in = [
        jnp.concatenate([twice(section(fac_left, i)), w_in[i]], axis=0) for i in range(layers)
    ]
    stacked_out = [jnp.pad(w_out[i], ((SIDE, 0), (0, 0))) for i in range(layers)]
    rights = [section(right_perturb_factors, i) for i in range(layers)]
    padded_right = [
        jnp.pad(twice(r), ((0, TILE - SIDE), (SIDE, 0))) for r in rights
    ]

    base = share(block[0], (*NEAR, FAR), tok)
    natural = jnp.swapaxes(base.reshape(nn, nf, width), 0, 1).reshape(tok, width)
    after = jnp.concatenate([natural[1:], jnp.zeros((1, width), BF)], axis=0)
    after = jnp.swapaxes(after.reshape(nf, nn, width), 0, 1).reshape(tok, width)
    place = jnp.arange(tok)
    token = (place % nf) * nn + place // nf
    weighting = jnp.where(token < tok - 1, 1.0 + 2.0 * token.astype(F32) / (tok - 2), 0.0)
    target = jnp.repeat(after, members, axis=0)
    row_weight = jnp.repeat(weighting, members)
    row_member = jnp.arange(rows) % members
    lane = jnp.arange(TILE)
    pick = (row_member[:, None] == (lane % HALF // rank)[None]) & (lane % HALF < low_lanes)[None]
    pick = pick.astype(F32)
    chunk = rows // ns
    own_member = jnp.arange(chunk) % members
    own_weight = lax.dynamic_slice(row_weight, (seg * chunk,), (chunk,))
    to_member = (own_member[None] == jnp.arange(members)[:, None]).astype(F32)

    group = nf * members
    scores = []
    stream = jnp.repeat(base, members, axis=0)
    for layer in range(layers):
        gain = gains[layer]
        if layer == 0:
            parts = swap(first(base, gain[None], stacked_in[0], low_lanes, ns), SEG)
            total = jnp.sum(parts.astype(F32), axis=0)
            extras = total[:, :HALF] + total[:, HALF:SIDE]
            hidden = total[:, SIDE:]
            scale = lax.rsqrt(extras[:, low_lanes : low_lanes + 1] / D + EPS)
            low = extras[:, :low_lanes].reshape(tok, members, rank)
            mixed = scale[:, None] * (
                hidden[:, None]
                + jnp.einsum(
                    "tmr,mrf->tmf",
                    low,
                    rights[0].reshape(members, rank, hid).astype(F32),
                    precision=lax.Precision.HIGHEST,
                )
            )
            gated = jax.nn.silu(mixed).astype(BF).reshape(rows, hid)
            update = jnp.dot(gated, w_out[layer], preferred_element_type=F32).astype(BF)
        else:
            part = enter(stream, gain[None], target, pick, stacked_in[layer], low_lanes)
            part = swap(part.reshape(ns, chunk, -1), SEG)
            gated, side = middle(part, padded_right[layer], low_lanes)
            scores.append(jnp.sum(to_member * (side[:, 0] * own_weight), axis=1))
            update = leave(swap(gated, SEG).reshape(rows, -1), stacked_out[layer])
        part = swap(update.reshape(nn, group, width), NEAR)
        part = jnp.sum(part.astype(F32), axis=0).astype(BF)
        parts = share(part, FAR, nf).reshape(nf, group, width)
        held = lax.dynamic_slice(stream, (near * group, 0), (group, width))
        fresh = (held.astype(F32) + jnp.sum(parts.astype(F32), axis=0)).astype(BF)
        if layer < layers - 1:
            stream = share(fresh, NEAR, nn).reshape(rows, width)

    wide = fresh.astype(F32)
    own_target = lax.dynamic_slice(target, (near * group, 0), (group, width)).astype(F32)
    once = jnp.where(near == 0, 1.0, 0.0)
    sums = jnp.concatenate(
        [
            jnp.sum(wide * wide, axis=1),
            jnp.sum(wide * own_target, axis=1),
            *[once * s for s in scores],
        ]
    )
    got = share(sums, ("x", *SEG), nx * ns).reshape(nx, ns, -1)
    got = jnp.sum(got, axis=1)
    square, along = got[:, :group], got[:, group : 2 * group]
    near_here = near // nx * nx + jnp.arange(nx)
    tokens = (jnp.arange(group) // members)[None] * nn + near_here[:, None]
    weights = jnp.where(tokens < tok - 1, 1.0 + 2.0 * tokens.astype(F32) / (tok - 2), 0.0)
    each = along * lax.rsqrt(square / D + EPS) * weights
    latest = jnp.sum(each.reshape(nx * nf, members), axis=0)
    both = jnp.concatenate([jnp.sum(got[:, 2 * group :], axis=0), latest])
    both = jnp.sum(share(both, ("h", "l"), nn // nx).reshape(nn // nx, -1), axis=0)
    mine = lax.dynamic_slice(fresh.reshape(nf, members, width), (far, 0, 0), (1, members, width))
    return both.reshape(layers, members) / math.sqrt((tok - 1) * D), mine


def solution(mesh):
    split = Mesh(mesh.devices.reshape(4, 2, 2, 4, 4, 2), (FAR, *NEAR, *SEG))
    pop = (FAR, *NEAR)
    return jax.shard_map(
        local,
        mesh=split,
        in_specs=(
            P(pop, SEG),
            P(None, pop, SEG),
            P(None, pop, SEG),
            P(None, SEG),
            P(None, None, None, SEG),
            P(None, None, None, pop),
            P(),
        ),
        out_specs=(P(), P(pop, None, SEG)),
        check_vma=False,
    )
```
